32 devices in a mesh: dp: 8 (over z, x), grp: 4 (over y, core).
Axes of the slice: x: 2, y: 2, z: 4, core: 2. Of those that a mesh axis runs over, the one named last changes fastest.
Arguments:
- inputs: bfloat16 [256, 128, 512], P(('dp', 'grp')), may hold values from -6 to 6
- top_down: bfloat16 [256, 128, 512], P(('dp', 'grp')), may hold values from -6 to 6
- lower_bounds: int32 [256, 128], P(('dp', 'grp')), may hold values 0 or 1
- h_init: float32 [256, 512], P(('dp', 'grp')), may hold values from -3 to 3
- c_init: float32 [256, 512], P(('dp', 'grp')), may hold values from -4 to 4
- z_init: float32 [256], P(('dp', 'grp')), may hold values from 0.1 to 0.9
- out_cot: bfloat16 [256, 128, 512], P(('dp', 'grp')), may hold values from -6 to 6
- gate_weight: float32 [1536, 2048], P('dp'), may hold values from -0.25 to 0.25
- gate_m: float32 [1536, 2048], P('dp'), may hold values from -4 to 4
- gate_v: float32 [1536, 2048], P('dp'), may hold values from 0.08192 to 0.32768
- small_params: float32 [5632], replicated, may hold values from -3 to 3
- small_m: float32 [5632], replicated, may hold values from -8.0453038 to 8.0453038
- small_v: float32 [5632], replicated, may hold values from 0.1605632 to 1.31072
Outputs:
- hidden_seq: bfloat16 [256, 128, 512], P(('dp', 'grp'))
- cell_last: float32 [256, 512], P(('dp', 'grp'))
- bounds_seq: float32 [256, 128], P(('dp', 'grp'))
- input_grad: float32 [256, 128, 512], P(('dp', 'grp'))
- weight_new: float32 [1536, 2048], P('dp')
- weight_m: float32 [1536, 2048], P('dp')
- weight_v: float32 [1536, 2048], P('dp')
- small_new: float32 [5632], replicated
- small_m_new: float32 [5632], replicated
- small_v_new: float32 [5632], replicated
The draws below stay inside these ranges and needn't reach their ends.
All inputs are finite; a program needn't handle non-finite values. No bound on the sum of `lower_bounds` on one device may be relied on, other than what follows from the above.
Results may differ from the reference program's by a relative error of at most 0.0061.
Values may be sent and summed in bfloat16 or wider, within the bound.
No kernel may reach another device: no remote copies, remote signals or barrier semaphores. Data moves between devices by JAX's collectives and lax.ppermute only.
A program may use at most 192 MiB of HBM per device.

```python
import math
import jax
import jax.numpy as jnp
from jax import lax

H = 512
G = 2048
SMALL = 5632
LEN = 128
BLK = 64
STEP = 10
WINDOWS = 256


def spread_scales(gate_scale, bound_scale):
    return jnp.concatenate([jnp.full((2 * G,), gate_scale, jnp.float32), jnp.full((3 * H,), bound_scale, jnp.float32)])


def draw_small_params(key, part):
    key = jax.random.fold_in(key, 11)
    key_gain, key_bias, key_bound = jax.random.split(key, 3)
    gains_part = jnp.clip(1.0 + 0.15 * jax.random.normal(key_gain, (G,), jnp.float32), 0.5, 1.5)
    biases_part = jnp.clip(0.5 * jax.random.normal(key_bias, (G,), jnp.float32), -3.0, 3.0)
    bound_part = jnp.clip(1.5 * (3 * H) ** (-0.5) * jax.random.normal(key_bound, (3 * H,), jnp.float32), -1.0, 1.0)
    return jnp.concatenate([gains_part, biases_part, bound_part])


def draw_small_m(key, part):
    key = jax.random.fold_in(key, 12)
    scale = (WINDOWS * LEN) ** 0.5 * spread_scales(0.1, 0.07) / 9.0
    return scale * jnp.clip(jax.random.normal(key, (SMALL,), jnp.float32), -4.0, 4.0)


def draw_small_v(key, part):
    key = jax.random.fold_in(key, 13)
    scales = spread_scales(0.1, 0.07)
    base = 0.001 * WINDOWS * LEN * scales * scales
    return base * jnp.exp(jax.random.uniform(key, (SMALL,), jnp.float32, 0.0, math.log(4.0)))


def with_ends(values, key, smallest, largest):
    dims = values.shape
    index_at = [jax.random.randint(jax.random.fold_in(key, axis), (), 0, dims[axis]) for axis in range(len(dims))]
    values = values.at[tuple(index_at)].set(smallest)
    longest = dims.index(max(dims))
    index_at[longest] = (index_at[longest] + 1) % dims[longest]
    return values.at[tuple(index_at)].set(largest)


def raised(result, rng, source, target, blocks, factor):
    owner, partner = [(jnp.arange(result.shape[position]) // (result.shape[position] // blocks)).reshape([-1 if axis == position else 1 for axis in range(result.ndim)]) for position in (source, target)]
    chosen = jax.random.permutation(rng, blocks)[partner]
    strong = (owner == chosen) | (owner == (partner + blocks // 2) % blocks)
    return jnp.where(strong, factor * result, result)


def block_scale(key, extent, pieces, smallest, high):
    gain, own = 1.0, jax.random.fold_in(key, 6)
    for dim, parts in pieces:
        draws = jnp.exp(jax.random.uniform(jax.random.fold_in(own, dim), (parts,), jnp.float32, smallest / len(pieces), high / len(pieces)))
        gain = gain * jnp.repeat(draws, extent[dim] // parts).reshape([-1 if axis == dim else 1 for axis in range(len(extent))])
    return gain


def centred(rng, extent, scale, reach, cuts=(), held_as=jnp.bfloat16):
    result = scale * jax.random.normal(rng, extent, jnp.float32)
    if cuts:
        result = result * block_scale(rng, extent, cuts, -0.22, 0.18)
    return jnp.clip(result, -reach, reach).astype(held_as)


def noise_with(stream_key, extent, scale, bound, pieces, heavy, kind=jnp.bfloat16):
    entries = scale * jax.random.normal(stream_key, extent, jnp.float32)
    if pieces:
        entries = entries * block_scale(stream_key, extent, pieces, -0.22, 0.18)
    return jnp.clip(raised(entries, jax.random.fold_in(stream_key, 3), *heavy), -bound, bound).astype(kind)


def setup_inputs(seed: int = 0) -> dict:
    seeds = jax.random.split(jax.random.key(seed), 14)
    inputs = noise_with(seeds[0], (WINDOWS, LEN, H), 1.0, 6.0, ((0, 32),), (0, 2, 32, 2.75))
    top_down = centred(seeds[1], (WINDOWS, LEN, H), 1.0, 6.0, ((0, 32),))
    lower_bounds = with_ends((jax.random.randint(seeds[2], (WINDOWS, LEN), 0, 5) < 2).astype(jnp.int32), jax.random.fold_in(seeds[2], 1), 0, 1)
    h_init = centred(seeds[3], (WINDOWS, H), 0.5, 3.0, ((0, 32),), jnp.float32)
    c_init = centred(seeds[4], (WINDOWS, H), 1.0, 4.0, ((0, 32),), jnp.float32)
    z_init = jnp.clip(0.1 + 0.79999997 * jax.random.uniform(seeds[5], (WINDOWS,), jnp.float32) ** block_scale(seeds[5], (WINDOWS,), ((0, 32),), -0.2, 0.2), 0.1, 0.9)
    out_cot = centred(seeds[6], (WINDOWS, LEN, H), 1.0, 6.0, ((0, 32),))
    gate_weight = centred(seeds[7], (3 * H, G), H ** -0.5, 0.25, ((0, 8),), jnp.float32)
    gate_m = centred(seeds[8], (3 * H, G), (0.05 * (WINDOWS * LEN) ** 0.5 / 9), 4.0, ((0, 8),), jnp.float32)
    gate_v = jnp.clip(jnp.exp(math.log(0.32768) - 1.3862944 * jax.random.uniform(seeds[9], (3 * H, G), jnp.float32) ** block_scale(seeds[9], (3 * H, G), ((0, 8),), -0.2, 0.2)), 0.08192, 0.32768)
    small_params = draw_small_params(jax.random.fold_in(seeds[13], 71), 0)
    small_m = draw_small_m(jax.random.fold_in(seeds[13], 71), 0)
    small_v = draw_small_v(jax.random.fold_in(seeds[13], 71), 0)
    return dict(inputs=inputs, top_down=top_down, lower_bounds=lower_bounds, h_init=h_init, c_init=c_init, z_init=z_init, out_cot=out_cot, gate_weight=gate_weight, gate_m=gate_m, gate_v=gate_v, small_params=small_params, small_m=small_m, small_v=small_v)


beta_first = 0.9
beta_second = 0.999
epsilon = 1e-08
weight_rate = 0.05
small_rate = 0.1
decay_rate = 0.1

@jax.custom_vjp
def low(v):
    return lax.optimization_barrier(v.astype(jnp.bfloat16)).astype(jnp.float32)

@jax.custom_vjp
def low_back(v):
    return v

def low_keep(v):
    return (low(v), None)

def low_pass(kept, grad):
    return (grad,)

def back_keep(v):
    return (v, None)

def back_low(kept, grad):
    return (low(grad),)
low.defvjp(low_keep, low_pass)
low_back.defvjp(back_keep, back_low)

def update_cell(recurrent, from_input, from_top, rounded, h, c, z, norm_gain, norm_bias, v_recur, bound_t, reach_input, reach_top):
    units = h.shape[1]
    z_col = z[:, None]
    b_col = bound_t[:, None]
    summed = b_col * from_input + recurrent + z_col * from_top
    centre = summed - lax.optimization_barrier(jnp.mean(summed, axis=-1, keepdims=True))
    spread = lax.optimization_barrier(jnp.mean(centre * centre, axis=-1, keepdims=True))
    normed = centre * lax.rsqrt(spread + 1e-05) * norm_gain + norm_bias
    forget = jax.nn.sigmoid(normed[:, :units])
    inward = jax.nn.sigmoid(normed[:, units:2 * units])
    outward = jax.nn.sigmoid(normed[:, 2 * units:3 * units])
    candidate = jnp.tanh(normed[:, 3 * units:])
    boundary = bound_t * reach_input + lax.optimization_barrier(jnp.sum(rounded * v_recur, axis=-1)) + z * reach_top
    z_next = jax.nn.sigmoid(boundary)
    copied = (1.0 - z_col) * (1.0 - b_col)
    written = inward * candidate
    c_next = z_col * written + (1.0 - z_col) * b_col * (forget * c + written) + copied * c
    h_next = (1.0 - copied) * outward * jnp.tanh(c_next) + copied * h
    return (h_next, c_next, z_next)

def forward(weight, small, inputs_f, top_f, bounds, h_start, c_start, z_start):
    highest = lax.Precision.HIGHEST
    weight_low = low(weight)
    w_input = weight_low[:H]
    w_recur = weight_low[H:2 * H]
    w_top = weight_low[2 * H:]
    norm_gain = small[:G]
    norm_bias = small[G:2 * G]
    v_input = small[2 * G:2 * G + H]
    v_recur = small[2 * G + H:2 * G + 2 * H]
    v_top = small[2 * G + 2 * H:]
    from_input = low_back(jnp.einsum('wth,hg->twg', inputs_f, w_input, precision=highest))
    from_top = low_back(jnp.einsum('wth,hg->twg', top_f, w_top, precision=highest))
    reach_input = lax.optimization_barrier(jnp.sum(inputs_f * v_input, axis=-1)).T
    reach_top = lax.optimization_barrier(jnp.sum(top_f * v_top, axis=-1)).T
    bounds_t = bounds.T
    blocks = LEN // BLK

    def by_blocks(array):
        return array.reshape((blocks, BLK) + array.shape[1:])

    def advance(carried, step_in):
        h, c, z = carried
        input_t, top_t, bound_t, reach_in_t, reach_top_t = step_in
        rounded = low(h)
        recurrent = low_back(jnp.dot(rounded, w_recur, precision=highest))
        h_next, c_next, z_next = update_cell(recurrent, input_t, top_t, rounded, h, c, z, norm_gain, norm_bias, v_recur, bound_t, reach_in_t, reach_top_t)
        return ((h_next, c_next, z_next), (h_next, z_next))

    @jax.checkpoint
    def run_block(carried, block_in):
        return lax.scan(advance, carried, block_in)
    carried, (hidden_steps, bound_steps) = lax.scan(run_block, (h_start, c_start, z_start), (by_blocks(from_input), by_blocks(from_top), by_blocks(bounds_t), by_blocks(reach_input), by_blocks(reach_top)))
    hidden_steps = hidden_steps.reshape((LEN,) + hidden_steps.shape[2:]).transpose(1, 0, 2)
    bound_steps = bound_steps.reshape((LEN,) + bound_steps.shape[2:]).T
    return (hidden_steps, carried[1], bound_steps)

def adam_update(master, gradient, first_moment, second_moment, step_rate, weight_decay):
    m = beta_first * first_moment + (1.0 - beta_first) * gradient
    v = beta_second * second_moment + (1.0 - beta_second) * gradient * gradient
    m_hat = m / (1.0 - beta_first ** STEP)
    v_hat = v / (1.0 - beta_second ** STEP)
    updated = master - step_rate * (m_hat / (jnp.sqrt(v_hat) + epsilon) + weight_decay * master)
    return (updated, m, v)

def reference(inputs, top_down, lower_bounds, h_init, c_init, z_init, out_cot, gate_weight, gate_m, gate_v, small_params, small_m, small_v):
    group_size = math.gcd(WINDOWS, max(1, 4096 // LEN))
    group_count = WINDOWS // group_size

    def window_slice(array, index):
        return lax.dynamic_slice_in_dim(array, (index * group_size).astype(jnp.int32), group_size, 0)

    def one_group(totals, index):
        inputs_f = window_slice(inputs, index).astype(jnp.float32)
        top_f = window_slice(top_down, index).astype(jnp.float32)
        bounds = window_slice(lower_bounds, index).astype(jnp.float32)
        h_start = window_slice(h_init, index)
        c_start = window_slice(c_init, index)
        z_start = window_slice(z_init, index)
        cotangent = window_slice(out_cot, index).astype(jnp.float32)

        def local_forward(weight, small, inputs_in):
            return forward(weight, small, inputs_in, top_f, bounds, h_start, c_start, z_start)
        (hidden_steps, cell_state, bound_steps), pullback = jax.vjp(local_forward, gate_weight, small_params, inputs_f)
        grad_weight, grad_small, grad_input = pullback((cotangent, jnp.zeros_like(cell_state), jnp.zeros_like(bound_steps)))
        return ((totals[0] + grad_weight, totals[1] + grad_small), (hidden_steps.astype(jnp.bfloat16), cell_state, bound_steps, grad_input))
    start = (jnp.zeros_like(gate_weight), jnp.zeros_like(small_params))
    (grad_weight, grad_small), (hidden_all, cell_all, bound_all, grad_all) = lax.scan(one_group, start, jnp.arange(group_count, dtype=jnp.int32))
    hidden_seq = hidden_all.reshape((WINDOWS, LEN, H))
    cell_last = cell_all.reshape((WINDOWS, H))
    bounds_seq = bound_all.reshape((WINDOWS, LEN))
    input_grad = grad_all.reshape((WINDOWS, LEN, H))
    weight_new, weight_m, weight_v = adam_update(gate_weight, grad_weight, gate_m, gate_v, weight_rate, decay_rate)
    small_new, small_m_new, small_v_new = adam_update(small_params, grad_small, small_m, small_v, small_rate, 0.0)
    return (hidden_seq, cell_last, bounds_seq, input_grad, weight_new, weight_m, weight_v, small_new, small_m_new, small_v_new)
```

```python
import functools

import jax
import jax.numpy as jnp
from jax import lax
from jax.experimental import pallas as pl
from jax.experimental.pallas import tpu as pltpu
from jax.sharding import PartitionSpec as P

STEP = 10
TIME_BLOCK = 64
LANES = 128
VMEM_LIMIT = 60 * 1024 * 1024
CORE = 1
PLANE = 2
Z_SIZE = 4
BY_HAND = True
SMALL_VMEM = 16 * 1024 * 1024


beta_first = 0.9
beta_second = 0.999
epsilon = 1e-08
weight_rate = 0.05
small_rate = 0.1
decay_rate = 0.1

f32 = jnp.float32
bf16 = jnp.bfloat16


def adam_update(master, gradient, first_moment, second_moment, step_rate, weight_decay):
    m = beta_first * first_moment + (1.0 - beta_first) * gradient
    v = beta_second * second_moment + (1.0 - beta_second) * gradient * gradient
    m_hat = m / (1.0 - beta_first**STEP)
    v_hat = v / (1.0 - beta_second**STEP)
    updated = master - step_rate * (m_hat / (jnp.sqrt(v_hat) + epsilon) + weight_decay * master)
    return (updated, m, v)


def wide(column, count):
    return jnp.concatenate([column] * count, axis=1)


def lane_sum(array):
    return jnp.sum(array, axis=-1, keepdims=True)


def half_sigmoid(half):
    return 0.5 * jnp.tanh(half) + 0.5


def fold(array, units):
    parts = [array[:, at : at + units] for at in range(0, array.shape[1], units)]
    while len(parts) > 1:
        parts = [a + b for a, b in zip(parts[::2], parts[1::2])]
    return parts[0]


def lane_start(value):
    return pl.multiple_of(value, LANES)


def own_place():
    group, owner = lax.axis_index("grp"), lax.axis_index("dp")
    return lax.rem(group, 2), group // 2, lax.rem(owner, 2), owner // 2


def part_columns(place, width, side, chunk):
    core, plane = place[:2]
    core = core if side == 0 else 1 - core
    first = core * (width // 2) + chunk * (width // 4)
    small = width // 16
    offsets = (1 - plane, plane, 2 + plane, 3 - plane)
    return [lane_start(first + offset * small) for offset in offsets]


def weight_pieces(place, width, pieces):
    core, plane, x, z = place
    for index, (piece, blocks) in enumerate(pieces):
        if piece is None:
            yield index, 0, 0, 0
            continue
        far_core, far_plane, far_x, first = piece
        column = (1 - core if far_core else core) * (width // 2)
        column = column + (1 - plane if far_plane else plane) * (width // 4) + first
        for block in range(blocks):
            row = lax.rem(z - block + blocks, blocks) * 2 + (1 - x if far_x else x)
            yield index, block, row, lane_start(column)


TILE = 256
UNITS = 2


class Columns:
    def __init__(self, ref, first, rows):
        self.ref, self.first, self.shape = ref, first, (rows, ref.shape[0] * LANES)

    def tile(self, row, rows, column, lanes):
        row = self.first + row
        parts = [self.ref[at // LANES, row : row + rows, :] for at in range(column, column + lanes, LANES)]
        return jnp.concatenate(parts, axis=1)

    def all(self):
        return self.tile(0, self.shape[0], 0, self.shape[1])

    def store(self, row, column, value):
        for at in range(0, value.shape[1], LANES):
            rows = slice(self.first + row, self.first + row + value.shape[0])
            self.ref[(column + at) // LANES, rows, :] = value[:, at : at + LANES]


class ByHand:
    def __init__(self, weights, order, transpose, accumulators):
        self.weights, self.order, self.transpose = weights, order, transpose
        self.accumulators = accumulators

    def push(self, index):
        for unit in range(UNITS):
            rows, columns, _, _ = self.order[unit][index % len(self.order[unit])]
            tile = self.weights.tile(rows, TILE, columns, TILE)
            pltpu.matmul_push_rhs(tile, index % 2, unit, transpose=self.transpose)

    def begin(self, rows):
        self.push(0)
        self.push(1)
        self.load_first(rows)

    def load_first(self, rows):
        nothing = jnp.zeros((2 * rows, TILE), bf16)
        for unit in range(UNITS):
            pltpu.matmul_acc_lhs(self.accumulators[unit][0], nothing, load_staged_rhs=0)
        self.push(2)

    def multiply(self, left, index):
        for unit in range(UNITS):
            _, _, depth, column = self.order[unit][index]
            part = left[:, depth * TILE : (depth + 1) * TILE]
            staged = None if index == 0 else index % 2
            pltpu.matmul_acc_lhs(self.accumulators[unit][column], part, load_staged_rhs=staged)

    def pop(self, column):
        return [pltpu.matmul_pop(self.accumulators[unit][column]) for unit in range(UNITS)]

    def product(self, left):
        rows = left.shape[0]
        left = jnp.concatenate([left, jnp.zeros_like(left)], axis=0).astype(bf16)
        parts = []
        count = len(self.order[0])
        for index in range(count):
            self.multiply(left, index)
            if index > 0:
                self.push(index + 2)
            column = self.order[0][index][3]
            if index + 1 == count or self.order[0][index + 1][3] != column:
                parts += [part[:rows] for part in self.pop(column)]
        self.load_first(rows)
        return jnp.concatenate(parts, axis=1)

    def end(self, rows):
        left = jnp.zeros((2 * rows, TILE * (1 + max(entry[2] for entry in self.order[0]))), bf16)
        for index in range(3):
            self.multiply(left, index)
        for column in sorted({entry[3] for entry in self.order[0][:3]}):
            self.pop(column)


class ByCompiler:
    def __init__(self, weights, transpose):
        self.weights, self.transpose = weights, transpose

    def begin(self, rows):
        pass

    def product(self, left):
        dims = (((1,), (1 if self.transpose else 0,)), ((), ()))
        return lax.dot_general(left.astype(bf16), self.weights.all(), dims, preferred_element_type=f32)

    def end(self, rows):
        pass


def block_product(left_ref, weights, out):
    if not BY_HAND:
        out[...] = jnp.dot(left_ref[...], weights.all(), preferred_element_type=f32)
        return
    rows = left_ref.shape[0]
    depth, columns = weights.shape[0] // TILE, weights.shape[1] // TILE // UNITS
    count = depth * columns

    def body(accumulators):
        def tile(index, unit):
            return index % depth * TILE, (index // depth * UNITS + unit) * TILE

        def push(index):
            for unit in range(UNITS):
                row, column = tile(index, unit)
                part = weights.tile(row, TILE, column, TILE)
                pltpu.matmul_push_rhs(part, index % 2, unit)

        push(0)
        push(1)
        for index in range(count):
            for unit in range(UNITS):
                row, column = tile(index, unit)
                accumulator = accumulators[unit][index // depth % 2]
                pltpu.matmul_acc_lhs(accumulator, left_ref[:, row : row + TILE], load_staged_rhs=index % 2)
            if index + 2 < count:
                push(index + 2)
            if index % depth == depth - 1:
                for unit in range(UNITS):
                    row, column = tile(index, unit)
                    out[:, column : column + TILE] = pltpu.matmul_pop(accumulators[unit][index // depth % 2])

    pl.run_scoped(body, [[pltpu.ACC(unit)((rows, TILE), f32) for _ in range(2)] for unit in range(UNITS)])


def transpose(array, out):
    if not BY_HAND:
        out.store(0, 0, array.all().T)
        return
    high, columns = array.shape[0] // TILE // UNITS, array.shape[1] // TILE
    count = high * columns
    diagonal = lax.broadcasted_iota(jnp.int32, (TILE, TILE), 0) == lax.broadcasted_iota(
        jnp.int32, (TILE, TILE), 1
    )
    identity = jnp.where(diagonal, 1.0, 0.0).astype(bf16)

    def body(accumulators):
        def tile(index, unit):
            return (index // columns * UNITS + unit) * TILE, index % columns * TILE

        def push(index):
            for unit in range(UNITS):
                row, column = tile(index, unit)
                part = array.tile(row, TILE, column, TILE)
                pltpu.matmul_push_rhs(part, index % 2, unit, transpose=True)

        push(0)
        push(1)
        for index in range(count):
            for unit in range(UNITS):
                pltpu.matmul_acc_lhs(accumulators[unit][index % 2], identity, load_staged_rhs=index % 2)
            if index + 2 < count:
                push(index + 2)
            for unit in range(UNITS):
                row, column = tile(index, unit)
                part = pltpu.matmul_pop(accumulators[unit][index % 2])
                out.store(column, row, part.astype(bf16))

    pl.run_scoped(body, [[pltpu.ACC(unit)((TILE, TILE), f32) for _ in range(2)] for unit in range(UNITS)])


def matrix_product(body, weights, rows, transpose):
    if not BY_HAND:
        return body(ByCompiler(weights, transpose))
    high, wide_ = weights.shape
    depth, columns = (wide_ // TILE, high // TILE) if transpose else (high // TILE, wide_ // TILE)
    order = []
    for unit in range(UNITS):
        places = [(k, column) for column in range(columns // UNITS) for k in range(depth)]
        entries = []
        for k, column in places:
            at = (k * TILE, (column * UNITS + unit) * TILE)
            entries.append((*(at[::-1] if transpose else at), k, column))
        order.append(entries)
    shapes = [
        [pltpu.ACC(unit)((2 * rows, TILE), f32) for _ in range(columns // UNITS)] for unit in range(UNITS)
    ]
    return pl.run_scoped(
        lambda accumulators: body(ByHand(weights, order, transpose, accumulators)), shapes
    )


def sweep_kernel(
    rows,
    blocks,
    pieces,
    *refs,
):
    place = own_place()
    piece_refs, refs = refs[: len(pieces)], refs[len(pieces) :]
    (
        xb_ref,
        top_ref,
        cot_ref,
        bound_ref,
        z0_ref,
        h0_ref,
        c0_ref,
        small_ref,
        left_ref,
        hidden_ref,
        clast_ref,
        bounds_ref,
        w_parts_ref,
        own0_ref,
        own1_ref,
        other0_ref,
        other1_ref,
        dl_ref,
        gsmall_ref,
        w_ref,
        wt_s,
        xhat_s,
        gate_s,
        ftop_s,
        cell_s,
        tanh_s,
        hprev_s,
        bound_s,
        ds_s,
        zpre_s,
        zpost_s,
        rstd_s,
        rin_s,
        rtop_s,
        gain_s,
        gain_half_s,
        bias_half_s,
        vrec_s,
        wbar_s,
        sgain_s,
        sbias_s,
        svec_s,
        h_s,
        c_s,
        z_s,
        seq_s,
        in_sems,
        out_sems,
    ) = refs
    units = xb_ref.shape[1]
    width = w_ref.shape[0] * LANES
    tiles = units // LANES
    gate_tiles = width // LANES
    tokens = xb_ref.shape[0]
    pairs = tokens // (2 * rows)
    now = pl.program_id(0)
    forward = now < blocks
    block = jnp.where(forward, now, 2 * blocks - 1 - now)
    base = pl.multiple_of(block * tokens, tokens)
    part_refs = (own0_ref, own1_ref, other0_ref, other1_ref)
    part_blocks = [
        start // LANES for index in range(4) for start in part_columns(place, width, index // 2, index % 2)
    ]
    write_out = [
        pltpu.make_async_copy(
            w_ref.at[index, pl.ds(0, units), :], w_parts_ref.at[:, pl.ds(at * LANES, LANES)], out_sems.at[at]
        )
        for at, index in enumerate(part_blocks)
    ]

    lane = lax.broadcasted_iota(jnp.int32, (rows, LANES), 1)

    def vector(index):
        first = 2 * width + index * units
        return small_ref[:, first : first + units]

    @pl.when(now == 0)
    def _():
        copies = []
        for index, part, row, column in weight_pieces(place, width, pieces):
            ref = piece_refs[index]
            _, deep, lanes = ref.shape
            row = row * deep if isinstance(row, int) else pl.multiple_of(row * deep, deep)
            for at in range(lanes // LANES):
                source = ref.at[part, :, pl.ds(at * LANES, LANES)]
                into = w_ref.at[column // LANES + at, pl.ds(row, deep), :]
                copies.append(pltpu.make_async_copy(source, into, in_sems.at[len(copies)]))
        for copy in copies:
            copy.start()
        gain = jnp.broadcast_to(small_ref[:, :width], (rows, width))
        bias = jnp.broadcast_to(small_ref[:, width : 2 * width], (rows, width))
        split = 3 * units
        gain_s[...] = gain
        gain_half_s[:, :split] = (0.5 * width**0.5) * gain[:, :split]
        gain_half_s[:, split:] = width**0.5 * gain[:, split:]
        bias_half_s[:, :split] = 0.5 * bias[:, :split]
        bias_half_s[:, split:] = bias[:, split:]
        vrec_s[...] = jnp.broadcast_to(vector(1), (rows, units))
        h_s[...] = h0_ref[...]
        c_s[...] = c0_ref[...]
        row = lax.broadcasted_iota(jnp.int32, (rows, rows), 0)
        same = row == lax.broadcasted_iota(jnp.int32, (rows, rows), 1)
        z0 = jnp.where(same, jnp.broadcast_to(z0_ref[...], (rows, rows)), 0.0)
        z_s[...] = jnp.broadcast_to(lane_sum(z0), z_s.shape)
        seq_s[...] = jnp.zeros_like(seq_s)
        for copy in copies:
            copy.wait()
        for copy in write_out:
            copy.start()

        def row_means(matrix):
            matrix.begin(rows)
            wbar_s[...] = matrix.product(jnp.full((rows, width), 1.0 / width, f32))
            matrix.end(rows)

        matrix_product(row_means, Columns(w_ref, units, units), rows, True)

    def forward_step(matrix, local, h, c, z):
        at = pl.ds(pl.multiple_of(base + local, rows), rows)
        rec = matrix.product(h)
        low_f = h.astype(bf16).astype(f32)
        given = xhat_s[at, :] + wide(z, gate_tiles) * ftop_s[at, :]
        mean = lane_sum(low_f * wbar_s[...] + fold(given, units) * (1.0 / width))
        reach = lane_sum(low_f * vrec_s[...])
        b = bound_s[at, :]
        s = rec + (given - mean)
        squares = s * s
        parts = [fold(squares[:, at : at + units], LANES) for at in range(0, width, units)]
        root = lax.rsqrt(lane_sum(functools.reduce(jnp.add, parts)) + width * 1e-05)
        rstd = root * width**0.5
        half = (s * gain_half_s[...]) * root + bias_half_s[...]
        copied = (1.0 - z) * (1.0 - b)
        kept = (1.0 - z) * b
        fresh = wide(0.5 * (z + kept), tiles)
        half_c = wide(0.5 * kept, tiles) * c
        rest_c = half_c + wide(copied, tiles) * c
        gates = jnp.tanh(half)
        forget, inward, outward, candidate = (gates[:, k * units : (k + 1) * units] for k in range(4))
        c_next = (fresh * inward + fresh) * candidate + (forget * half_c + rest_c)
        th = jnp.tanh(c_next)
        forget, inward, outward = (0.5 * gate + 0.5 for gate in (forget, inward, outward))
        h_next = (wide(1.0 - copied, tiles) * outward) * th + wide(copied, tiles) * h
        z_next = half_sigmoid(0.5 * (rin_s[at, :] + reach + z * rtop_s[at, :]))
        xhat_s[at, :] = s * rstd
        gate_s[at, :units] = forget
        gate_s[at, units : 2 * units] = inward
        gate_s[at, 2 * units : 3 * units] = outward
        gate_s[at, 3 * units :] = candidate
        cell_s[at, :] = c
        tanh_s[at, :] = th
        hprev_s[at, :] = h
        zpre_s[at, :] = z
        zpost_s[at, :] = z_next
        rstd_s[at, :] = jnp.broadcast_to(rstd, z.shape)
        return h_next, c_next, z_next

    @pl.when(forward)
    def _():
        at = pl.ds(base, tokens)
        block_product(xb_ref, Columns(w_ref, 0, units), xhat_s.at[at, :])
        block_product(top_ref, Columns(w_ref, 2 * units, units), ftop_s.at[at, :])
        left_ref[:, :units] = xb_ref[...]
        shape = (tokens, LANES)
        rin_s[at, :] = jnp.broadcast_to(lane_sum(xb_ref[...].astype(f32) * vector(0)), shape)
        rtop_s[at, :] = jnp.broadcast_to(lane_sum(top_ref[...].astype(f32) * vector(2)), shape)
        for index in range(tokens // rows):
            column = lane_sum(jnp.where(lane == block * (tokens // rows) + index, bound_ref[...], 0.0))
            here = pl.ds(pl.multiple_of(base + index * rows, rows), rows)
            bound_s[here, :] = jnp.broadcast_to(column, (rows, LANES))

        def pair(matrix, index, carry):
            h0, c0, z0, seq = carry
            local = pl.multiple_of(index * 2 * rows, 2 * rows)
            h1, c1, z1 = forward_step(matrix, local, h0, c0, z0)
            h2, c2, z2 = forward_step(matrix, local + rows, h1, c1, z1)
            both = pl.ds(local, 2 * rows)
            left_ref[both, units : 2 * units] = jnp.concatenate([h0, h1], axis=0).astype(bf16)
            hidden_ref[both, :] = jnp.concatenate([h1, h2], axis=0).astype(bf16)
            z_pair = wide(jnp.concatenate([z0, z1], axis=0), tiles)
            left_ref[both, 2 * units :] = (top_ref[both, :].astype(f32) * z_pair).astype(bf16)
            step = block * (2 * pairs) + 2 * index
            seq = jnp.where(lane == step, z1, jnp.where(lane == step + 1, z2, seq))
            return h2, c2, z2, seq

        def steps(matrix):
            matrix.begin(rows)
            start = (h_s[...], c_s[...], z_s[...], seq_s[...])
            h, c, z, seq = lax.fori_loop(0, pairs, functools.partial(pair, matrix), start, unroll=4)
            matrix.end(rows)
            h_s[...] = h
            c_s[...] = c
            z_s[...] = z
            seq_s[...] = seq

        matrix_product(steps, Columns(w_ref, units, units), rows, False)

    @pl.when(now == blocks)
    def _():
        clast_ref[...] = c_s[...]
        bounds_ref[...] = seq_s[...]
        for copy in write_out:
            copy.wait()
        transpose(Columns(w_ref, units, units), Columns(wt_s, 0, width))
        h_s[...] = jnp.zeros_like(h_s)
        c_s[...] = jnp.zeros_like(c_s)
        z_s[...] = jnp.zeros_like(z_s)
        sgain_s[...] = jnp.zeros_like(sgain_s)
        sbias_s[...] = jnp.zeros_like(sbias_s)
        svec_s[...] = jnp.zeros_like(svec_s)

    def backward_step(matrix, local, cot, xb, top, bh_known, bh_mat, bc, bz):
        at = pl.ds(pl.multiple_of(base + local, rows), rows)
        z = zpre_s[at, :]
        b = bound_s[at, :]
        z_next = zpost_s[at, :]
        copied = (1.0 - z) * (1.0 - b)
        kept = (1.0 - z) * b
        fresh = z + kept
        c = cell_s[at, :]
        th = tanh_s[at, :]
        h = hprev_s[at, :]
        forget = gate_s[at, :units]
        inward = gate_s[at, units : 2 * units]
        outward = gate_s[at, 2 * units : 3 * units]
        candidate = gate_s[at, 3 * units :]
        xhat = xhat_s[at, :]
        rstd = rstd_s[at, :]
        new = wide(1.0 - copied, tiles) * outward
        written = inward * candidate
        by_dh = new * (1.0 - th * th)
        by_out = new * (th * (1.0 - outward))
        by_dc = (
            wide(kept, tiles) * c * (forget * (1.0 - forget)),
            wide(fresh, tiles) * (written * (1.0 - inward)),
            wide(fresh, tiles) * (inward * (1.0 - candidate * candidate)),
        )
        gain = [gain_s[:, k * units : (k + 1) * units] for k in range(4)]
        dh_known = bh_known + cot
        dh = dh_known + bh_mat
        dc = (bc + dh_known * by_dh) + bh_mat * by_dh
        d_out = dh * by_out
        dx_out = dh_known * (by_out * gain[2]) + bh_mat * (by_out * gain[2])
        dn = jnp.concatenate([dc * by_dc[0], dc * by_dc[1], d_out, dc * by_dc[2]], axis=1)
        dx = jnp.concatenate(
            [dc * (by_dc[0] * gain[0]), dc * (by_dc[1] * gain[1]), dx_out, dc * (by_dc[2] * gain[3])], axis=1
        )
        rstd_wide = wide(rstd, gate_tiles)
        sum1 = lane_sum(fold(dx, units))
        sum2 = lane_sum(fold(dx * xhat, units))
        ds = (rstd_wide * dx - (rstd_wide * (1.0 / width)) * sum1) - (xhat * rstd_wide * (1.0 / width)) * sum2
        bh_mat = matrix.product(ds)
        d_logit = bz * (z_next * (1.0 - z_next))
        bh_known = wide(copied, tiles) * dh + wide(d_logit, tiles) * vrec_s[...]
        bc_next = dc * (wide(kept, tiles) * forget + wide(copied, tiles))
        by_z = dc * (written - wide(b, tiles) * (forget * c + written) - wide(1.0 - b, tiles) * c)
        by_z = by_z - wide(1.0 - b, tiles) * (dh * (h - outward * th))
        bz_next = lane_sum(fold(ds * ftop_s[at, :], units) + by_z) + d_logit * rtop_s[at, :]
        sgain_s[...] += dn * xhat
        sbias_s[...] += dn
        low = h.astype(bf16).astype(f32)
        svec_s[:, :units] += wide(d_logit, tiles) * xb
        svec_s[:, units : 2 * units] += wide(d_logit, tiles) * low
        svec_s[:, 2 * units :] += wide(d_logit * z, tiles) * top
        return ds, d_logit, (bh_known, bh_mat, bc_next, bz_next)

    @pl.when(jnp.logical_not(forward))
    def _():
        def pair(matrix, index, carry):
            local = pl.multiple_of((pairs - 1 - index) * 2 * rows, 2 * rows)
            both = pl.ds(local, 2 * rows)
            given = [ref[both, :].astype(f32) for ref in (cot_ref, xb_ref, top_ref)]
            seq, *carry = carry
            ds1, dl1, carry = backward_step(matrix, local + rows, *(array[rows:] for array in given), *carry)
            ds0, dl0, carry = backward_step(matrix, local, *(array[:rows] for array in given), *carry)
            ds = jnp.concatenate([ds0, ds1], axis=0).astype(bf16)
            for at in range(gate_tiles):
                ds_s[at, :, :] = ds[:, at * LANES : (at + 1) * LANES]
            for at, index in enumerate(part_blocks):
                part_refs[at // tiles][both, at % tiles * LANES : (at % tiles + 1) * LANES] = ds_s[index, :, :]
            step = (base + local) // rows
            seq = jnp.where(lane == step, dl0, jnp.where(lane == step + 1, dl1, seq))
            return (seq, *carry)

        def steps(matrix):
            matrix.begin(rows)
            start = (seq_s[...], h_s[...], jnp.zeros((rows, units), f32), c_s[...], z_s[...])
            seq, bh_known, bh_mat, bc, bz = lax.fori_loop(0, pairs, functools.partial(pair, matrix), start, unroll=4)
            matrix.end(rows)
            h_s[...] = bh_known + bh_mat
            c_s[...] = bc
            z_s[...] = bz
            seq_s[...] = seq

        matrix_product(steps, Columns(wt_s, 0, width), rows, False)

    @pl.when(now == 2 * blocks - 1)
    def _():
        dl_ref[...] = seq_s[...]
        gsmall_ref[...] = jnp.zeros_like(gsmall_ref)
        row = 0
        for ref in (sgain_s, sbias_s, svec_s):
            total = jnp.sum(ref[...], axis=0, keepdims=True)
            for at in range(0, total.shape[1], LANES):
                gsmall_ref[row : row + 1, :] = total[:, at : at + LANES]
                row += 1


def sweep(described, pieces, xb, top, cot, bounds, z0, h0, c0, small_params):
    tokens, units = xb.shape
    rows = h0.shape[0]
    width = 4 * units
    block = TIME_BLOCK * rows
    blocks = tokens // block
    small_rows = -(-small_params.shape[1] // (16 * LANES)) * 16

    def both_ways(lanes):
        return pl.BlockSpec((block, lanes), lambda i: (jnp.where(i < blocks, i, 2 * blocks - 1 - i), 0))

    def going(lanes):
        return pl.BlockSpec((block, lanes), lambda i: (jnp.minimum(i, blocks - 1), 0))

    def returning(lanes):
        return pl.BlockSpec((block, lanes), lambda i: (jnp.minimum(blocks - 1, 2 * blocks - 1 - i), 0))

    def whole(shape):
        return pl.BlockSpec(shape, lambda i: (0, 0))

    anywhere = pl.BlockSpec(memory_space=pl.ANY)
    outs = [
        (going(3 * units), (tokens, 3 * units), bf16),
        (going(units), (tokens, units), bf16),
        (whole((rows, units)), (rows, units), f32),
        (whole((rows, LANES)), (rows, LANES), f32),
        (anywhere, (units, width), bf16),
        *[(returning(units), (tokens, units), bf16)] * 4,
        (whole((rows, LANES)), (rows, LANES), f32),
        (whole((small_rows, LANES)), (small_rows, LANES), f32),
    ]
    constants = (bounds, z0, h0, c0, small_params)
    return pl.pallas_call(
        functools.partial(sweep_kernel, rows, blocks, described),
        grid=(2 * blocks,),
        in_specs=[anywhere] * len(pieces)
        + [both_ways(units), both_ways(units), returning(units)]
        + [whole(array.shape) for array in constants],
        out_specs=[spec for spec, _, _ in outs],
        out_shape=[jax.ShapeDtypeStruct(shape, dtype) for _, shape, dtype in outs],
        scratch_shapes=[
            pltpu.VMEM((width // LANES, 3 * units, LANES), bf16),
            pltpu.VMEM((units // LANES, width, LANES), bf16),
            *[pltpu.VMEM((tokens, width), f32)] * 3,
            *[pltpu.VMEM((tokens, units), f32)] * 3,
            pltpu.VMEM((tokens, LANES), f32),
            pltpu.VMEM((width // LANES, 2 * rows, LANES), bf16),
            *[pltpu.VMEM((tokens, LANES), f32)] * 5,
            *[pltpu.VMEM((rows, width), f32)] * 3,
            *[pltpu.VMEM((rows, units), f32)] * 2,
            *[pltpu.VMEM((rows, width), f32)] * 2,
            pltpu.VMEM((rows, 3 * units), f32),
            *[pltpu.VMEM((rows, units), f32)] * 2,
            *[pltpu.VMEM((rows, LANES), f32)] * 2,
            pltpu.SemaphoreType.DMA((sum(piece.shape[0] * piece.shape[2] // LANES for piece in pieces),)),
            pltpu.SemaphoreType.DMA((width // LANES,)),
        ],
        compiler_params=pltpu.CompilerParams(
            dimension_semantics=("arbitrary",), vmem_limit_bytes=VMEM_LIMIT
        ),
        cost_estimate=pl.CostEstimate(flops=130 * 10**9, bytes_accessed=10**8, transcendentals=0),
        name="sweep",
    )(*pieces, xb, top, cot, *constants)


def adam_kernel(chunk, *refs):
    grads, (w_ref, m_ref, v_ref), (*outs, new_s, sems) = refs[:4], refs[4:7], refs[-5:]
    core, plane, _, _ = own_place()
    quarter = w_ref.shape[1] // 4
    copies = []
    for side in range(2):
        start = (1 - core if side else core) * (2 * quarter) + chunk * quarter
        for far_plane in range(2):
            grad_ref = grads[2 * side + far_plane]
            lanes = grad_ref.shape[1] // 2
            for half in range(2):
                at = (2 * half + (1 - plane if far_plane else plane)) * lanes
                columns = pl.ds(lane_start(start + at), lanes)
                grad = grad_ref[:, half * lanes : (half + 1) * lanes].astype(f32)
                new = adam_update(
                    w_ref[:, columns], grad, m_ref[:, columns], v_ref[:, columns], weight_rate, decay_rate
                )
                for index, value in enumerate(new):
                    new_s[index, side, :, pl.ds(lane_start(at), lanes)] = value
        for index, ref in enumerate(outs):
            into = ref.at[:, pl.ds(lane_start(start), quarter)]
            copies.append(pltpu.make_async_copy(new_s.at[index, side], into, sems.at[index, side]))
            copies[-1].start()
    for copy in copies:
        copy.wait()


def adam_columns(chunk, grads, master, first_moment, second_moment, earlier):
    rows, width = master.shape
    in_vmem, anywhere = pl.BlockSpec(memory_space=pltpu.VMEM), pl.BlockSpec(memory_space=pl.ANY)
    return pl.pallas_call(
        functools.partial(adam_kernel, chunk),
        in_specs=[in_vmem] * 7 + [anywhere] * len(earlier),
        out_specs=[anywhere] * 3,
        out_shape=[jax.ShapeDtypeStruct(master.shape, f32)] * 3,
        scratch_shapes=[pltpu.VMEM((3, 2, rows, width // 4), f32), pltpu.SemaphoreType.DMA((3, 2))],
        input_output_aliases={7 + k: k for k in range(len(earlier))},
        compiler_params=pltpu.CompilerParams(vmem_limit_bytes=SMALL_VMEM),
        name="adam",
    )(*grads, master, first_moment, second_moment, *earlier)


def after(value, others):
    return lax.optimization_barrier((value, others))[0]


def swap(array, bit, axis="grp"):
    count = lax.axis_size(axis)
    return lax.ppermute(array, axis, [(index, index ^ bit) for index in range(count)])


def along_z(array, step):
    count = lax.axis_size("dp")
    return lax.ppermute(array, "dp", [(index, (index + 2 * step) % count) for index in range(count)])


def gather_weights(shard, core, plane, ready):
    width = shard.shape[1]
    count = lax.axis_size("dp")
    if count != Z_SIZE * 2:
        return (None,), (lax.all_gather(shard.astype(bf16), "dp", axis=0, tiled=True)[None],)
    quarter = width // 4
    lanes = quarter // 2
    half = lanes // 2
    firsts = (0, lanes)
    owns = [
        lax.dynamic_slice_in_dim(
            shard, core * (width // 2) + plane * quarter + first, lanes, axis=1
        ).astype(bf16)
        for first in firsts
    ]

    def line(own):
        return tuple(along_z(own, step) for step in range(1, Z_SIZE))

    def planes(own, arrived):
        mine = jnp.stack((own,) + arrived)
        return mine, swap(mine, 1, "dp"), swap(mine, PLANE)

    def corners(pieces):
        return pieces[1][..., :half], pieces[2][..., half:]

    def corner_swap(from_x, from_y):
        return swap(from_x, PLANE), swap(from_y, 1, "dp")

    arrived0 = line(owns[0])
    own1 = after(owns[1], arrived0)
    arrived1 = line(own1)
    pieces0 = planes(owns[0], after(arrived0, ready))
    corners0 = corners(pieces0)
    pieces1 = planes(own1, after(arrived1, corners0))
    corners1 = corners(pieces1)
    all_pieces = [pieces0 + corner_swap(*corners0), pieces1 + corner_swap(*corners1)]
    kinds, pieces = [], []
    for first, here in zip(firsts, all_pieces):
        for far_core in (False, True):
            kinds += [
                (far_core, False, False, first),
                (far_core, False, True, first),
                (far_core, True, False, first),
                (far_core, True, True, first),
                (far_core, True, True, first + half),
            ]
            pieces += [swap(piece, CORE) for piece in after(here, corners1)] if far_core else here
    return tuple(kinds), tuple(pieces)


def split(value):
    high = value.astype(bf16)
    return high, (value - high.astype(f32)).astype(bf16)


def joined(high, low):
    return high.astype(f32) + low.astype(f32)


def both_parts(value):
    return joined(*split(value))


def small_call(kernel, arrays, extra, outs, extra_out=False):
    arrays = [*arrays, *extra]
    if extra_out:
        outs = outs + [(array.shape, array.dtype) for array in extra]
    return pl.pallas_call(
        functools.partial(kernel, len(extra)),
        in_specs=[pl.BlockSpec(memory_space=pltpu.VMEM)] * len(arrays),
        out_specs=[pl.BlockSpec(memory_space=pltpu.VMEM)] * len(outs),
        out_shape=[jax.ShapeDtypeStruct(shape, dtype) for shape, dtype in outs],
        compiler_params=pltpu.CompilerParams(vmem_limit_bytes=SMALL_VMEM),
        name=kernel.__name__,
    )(*arrays)


def first_kernel(with_small, total_ref, *refs):
    small_refs, (to_y_ref, to_x_ref) = refs[:with_small], refs[with_small:]
    _, _, x, _ = own_place()
    _, _, rows, columns = total_ref.shape
    small = columns // 4
    for index in range(2 * Z_SIZE):
        to_y_ref[index * rows : (index + 1) * rows, :] = total_ref[index // 2, index % 2, :, :small].astype(bf16)
    if with_small:
        deep = small_refs[0].shape[0]
        start = 2 * Z_SIZE * rows
        high, low = split(small_refs[0][...])
        to_y_ref[start : start + deep, :] = high
        to_y_ref[start + deep :, :] = low
    to_x_ref[...] = total_ref[:, 1 - x, :, 2 * small :].astype(bf16)


def second_kernel(with_small, total_ref, from_y_ref, from_x_ref, *refs):
    small_refs, (to_x_ref, to_y_ref, kept_ref, *small_outs) = refs[:with_small], refs[with_small:]
    _, _, x, _ = own_place()
    _, _, rows, columns = total_ref.shape
    small = columns // 4
    middle = slice(small, 2 * small)

    def from_y(index, of_x):
        start = (2 * index + of_x) * rows
        if rows % 16 == 0:
            start = pl.multiple_of(start, 16)
        return from_y_ref[pl.ds(start, rows), :].astype(f32)

    for index in range(Z_SIZE):
        away = total_ref[index, 1 - x, :, middle] + from_y(index, 1 - x)
        to_x_ref[index * rows : (index + 1) * rows, :] = away.astype(bf16)
        kept_ref[index, :, :small] = total_ref[index, x, :, middle] + from_y(index, x)
    right = total_ref[:, x, :, 2 * small :] + from_x_ref[...].astype(f32)
    kept_ref[..., small:] = right[..., :small]
    to_y_ref[...] = right[..., small:].astype(bf16)
    if with_small:
        deep = small_refs[0].shape[0]
        start = 2 * Z_SIZE * rows
        arrived = joined(from_y_ref[start : start + deep, :], from_y_ref[start + deep :, :])
        value = both_parts(small_refs[0][...]) + arrived
        small_outs[0][...] = value
        start = Z_SIZE * rows
        high, low = split(value)
        to_x_ref[start : start + deep, :] = high
        to_x_ref[start + deep :, :] = low


def third_kernel(with_small, kept_ref, from_x_ref, from_y_ref, *refs):
    small_refs, (own_ref, *away_refs) = refs[:with_small], refs[with_small:]
    _, _, _, z = own_place()
    _, rows, columns = kept_ref.shape
    small = columns // 2
    small_outs, away_refs = away_refs[Z_SIZE - 1 :], away_refs[: Z_SIZE - 1]
    for step, ref in enumerate([own_ref] + away_refs):
        at = lax.rem(z + step, Z_SIZE)
        start = at * rows
        if rows % 16 == 0:
            start = pl.multiple_of(start, 16)
        left = kept_ref[at, :, :small] + from_x_ref[pl.ds(start, rows), :].astype(f32)
        ref[:rows, :small] = left.astype(ref.dtype)
        ref[:rows, small:] = (kept_ref[at, :, small:] + from_y_ref[at].astype(f32)).astype(ref.dtype)
    if with_small:
        deep = small_refs[0].shape[0]
        start = Z_SIZE * rows
        arrived = joined(from_x_ref[start : start + deep, :], from_x_ref[start + deep :, :])
        value = both_parts(small_refs[0][...]) + arrived
        small_outs[0][...] = value
        high, low = split(value)
        for ref in away_refs:
            ref[rows:, :small] = high
            ref[rows:, small:] = low


def fourth_kernel(with_small, own_ref, *refs):
    arrived, refs = refs[: Z_SIZE - 1], refs[Z_SIZE - 1 :]
    small_refs, (out_ref, *small_outs) = refs[:with_small], refs[with_small:]
    rows, columns = own_ref.shape
    small = columns // 2
    total = own_ref[...]
    for ref in arrived:
        total = total + ref[:rows, :].astype(f32)
    out_ref[...] = total.astype(bf16)
    if with_small:
        one, two, three = (joined(ref[rows:, :small], ref[rows:, small:]) for ref in arrived)
        value = (both_parts(small_refs[0][...]) + two) + (one + three)
        small_outs[0][:, :small], small_outs[0][:, small:] = split(value)


def reduce_rows(totals, grad_small, late, late_inputs):
    count = lax.axis_size("dp")
    all_rows, columns = totals[0].shape
    small = columns // 4
    deep = grad_small.shape[0]
    if count != Z_SIZE * 2:
        sums = []
        for total in totals:
            mine = lax.psum_scatter(total.astype(bf16), "dp", scatter_dimension=0, tiled=True).astype(f32)
            away = jnp.concatenate([mine[:, :small], mine[:, 3 * small :]], axis=1).astype(bf16)
            sums.append((mine[:, small : 3 * small] + swap(away, PLANE).astype(f32)).astype(bf16))
        total = grad_small + swap(grad_small, PLANE)
        bit = 1
        while bit < count:
            total = total + swap(total, bit, "dp")
            bit *= 2
        return sums, jnp.concatenate(split(total), axis=1), late(*late_inputs)
    rows = all_rows // count
    totals = [total.reshape(Z_SIZE, 2, rows, columns) for total in totals]

    def first(total, extra):
        below = 2 * deep if extra else 0
        outs = [((2 * Z_SIZE * rows + below, small), bf16), ((Z_SIZE, rows, 2 * small), bf16)]
        return small_call(first_kernel, [total], extra, outs)

    def first_swap(to_y, to_x):
        return swap(to_y, PLANE), swap(to_x, 1, "dp")

    def second(total, arrived, extra):
        below = 2 * deep if extra else 0
        outs = [
            ((Z_SIZE * rows + below, small), bf16),
            ((Z_SIZE, rows, small), bf16),
            ((Z_SIZE, rows, 2 * small), f32),
        ]
        return small_call(second_kernel, [total, *arrived], extra, outs, True)

    def second_swap(to_x, to_y, kept):
        return kept, swap(to_x, 1, "dp"), swap(to_y, PLANE)

    def third(arrived, extra):
        below = deep if extra else 0
        outs = [((rows, 2 * small), f32)] + [((rows + below, 2 * small), bf16)] * (Z_SIZE - 1)
        return small_call(third_kernel, arrived, extra, outs, True)

    def third_swap(own, *away):
        return (own,) + tuple(along_z(array, step + 1) for step, array in enumerate(away))

    def fourth(arrived, extra):
        outs = [((rows, 2 * small), bf16)] + [((deep, 2 * small), bf16)] * len(extra)
        return small_call(fourth_kernel, arrived, extra, outs)

    extra = [grad_small]
    out0 = first(totals[0], extra)
    in0 = first_swap(*out0)
    out1 = first(totals[1], [])
    in1 = first_swap(*out1)
    *out0, value = second(totals[0], in0, extra)
    extra = [value]
    in0 = second_swap(*out0)
    out1 = second(totals[1], after(in1, out0), [])
    in1 = second_swap(*out1)
    *out0, value = third(after(in0, out1), extra)
    extra = [value]
    in0 = third_swap(*out0)
    out1 = third(after(in1, out0), [])
    late_outputs = late(*after(late_inputs, out1))
    in1 = third_swap(*out1)
    sum0, small_pair = fourth(after(in0, (late_outputs, in1[1])), extra)
    (sum1,) = fourth(after(in1, sum0), [])
    return [sum0, sum1], small_pair, late_outputs


def shards(
    inputs,
    top_down,
    lower_bounds,
    h_init,
    c_init,
    z_init,
    out_cot,
    gate_weight,
    gate_m,
    gate_v,
    small_params,
    small_m,
    small_v,
):
    rows, steps, units = inputs.shape
    tokens = rows * steps
    width = 4 * units
    core, plane, _, _ = own_place()

    def by_time(array):
        return jnp.swapaxes(array, 0, 1).reshape((tokens,) + array.shape[2:])

    def by_window(array):
        return jnp.swapaxes(array.reshape((steps, rows) + array.shape[1:]), 0, 1)

    bound = by_time(lower_bounds).astype(f32)
    ready = (
        by_time(inputs) * bound[:, None].astype(bf16),
        by_time(top_down),
        by_time(out_cot),
        jnp.pad(lower_bounds.astype(f32), ((0, 0), (0, LANES - steps))),
        z_init[None],
        small_params[None],
    )
    kinds, pieces = gather_weights(gate_weight, core, plane, ready)
    described = tuple((kind, piece.shape[0]) for kind, piece in zip(kinds, pieces))
    xb, top, cot, bounds_f, z0, small_row = ready
    left, hidden, c_last, bounds, w_parts, own0, own1, other0, other1, d_logit, grad_small = sweep(
        described, pieces, xb, top, cot, bounds_f, z0, h_init, c_init, small_row
    )

    def product(right):
        return lax.dot_general(left, right, (((0,), (0,)), ((), ())), preferred_element_type=f32)

    totals = []
    for own, other in ((own0, other0), (own1, other1)):
        from_core = swap(product(other).astype(bf16), CORE)
        totals.append(product(own) + from_core.astype(f32))
    v_input = small_params[2 * width : 2 * width + units]

    def late(d_logit, hidden, *parts):
        by_input = 0.0
        for index, part in enumerate(parts):
            columns = w_parts[:, index * units : (index + 1) * units]
            by_input = by_input + lax.dot_general(
                part, columns, (((1,), (1,)), ((), ())), preferred_element_type=f32
            )
        by_logit = lower_bounds.astype(f32) * d_logit[:, :steps]
        input_grad = by_window(bound[:, None] * by_input) + by_logit[:, :, None] * v_input
        return by_window(hidden), input_grad

    late_inputs = d_logit, hidden, own0, own1, other0, other1
    sums, small_pair, (hidden, input_grad) = reduce_rows(totals, grad_small, late, late_inputs)
    weights = ()
    for chunk, grad in enumerate(sums):
        far = swap(grad, PLANE)
        grads = [grad, far, swap(after(grad, far), CORE), swap(grad, CORE | PLANE)]
        if chunk == 0:
            near_pair = swap(after(small_pair, far), CORE)
        weights = adam_columns(chunk, grads, gate_weight, gate_m, gate_v, weights)
    weight_new, weight_m, weight_v = weights
    small_total = 0.0
    for pair in (small_pair, near_pair):
        small_total = small_total + joined(pair[:, :LANES], pair[:, LANES:])
    small_total = small_total.reshape(-1)[: small_params.shape[0]]

    small_new, small_m_new, small_v_new = adam_update(
        small_params, small_total, small_m, small_v, small_rate, 0.0
    )
    return (
        hidden,
        c_last,
        bounds[:, :steps],
        input_grad,
        weight_new,
        weight_m,
        weight_v,
        small_new,
        small_m_new,
        small_v_new,
    )


def solution(mesh):
    def program(*arrays):
        with jax.sharding.use_abstract_mesh(mesh.abstract_mesh):
            return sharded(*arrays)

    tokens = P(("dp", "grp"), None, None)
    windows = P(("dp", "grp"), None)
    owned = P("dp", None)
    in_specs = (
        (tokens, tokens, windows, windows, windows, P(("dp", "grp")), tokens)
        + (owned,) * 3
        + (P(),) * 3
    )
    out_specs = (tokens, windows, windows, tokens) + (owned,) * 3 + (P(),) * 3
    sharded = jax.shard_map(shards, mesh=mesh, in_specs=in_specs, out_specs=out_specs, check_vma=False)
    return program
```

```python
import functools

import jax
import jax.numpy as jnp
from jax import lax
from jax.experimental import pallas as pl
from jax.experimental.pallas import tpu as pltpu
from jax.sharding import PartitionSpec as P

STEP = 10
TIME_BLOCK = 64
LANES = 128
VMEM_LIMIT = 60 * 1024 * 1024
CORE = 1
PLANE = 2
Z_SIZE = 4
BY_HAND = True
SMALL_VMEM = 16 * 1024 * 1024


beta_first = 0.9
beta_second = 0.999
epsilon = 1e-08
weight_rate = 0.05
small_rate = 0.1
decay_rate = 0.1

f32 = jnp.float32
bf16 = jnp.bfloat16


def adam_update(master, gradient, first_moment, second_moment, step_rate, weight_decay):
    m = beta_first * first_moment + (1.0 - beta_first) * gradient
    v = beta_second * second_moment + (1.0 - beta_second) * gradient * gradient
    m_hat = m / (1.0 - beta_first**STEP)
    v_hat = v / (1.0 - beta_second**STEP)
    updated = master - step_rate * (m_hat / (jnp.sqrt(v_hat) + epsilon) + weight_decay * master)
    return (updated, m, v)


def wide(column, count):
    return jnp.concatenate([column] * count, axis=1)


def lane_sum(array):
    return jnp.sum(array, axis=-1, keepdims=True)


def half_sigmoid(half):
    return 0.5 * jnp.tanh(half) + 0.5


def fold(array, units):
    parts = [array[:, at : at + units] for at in range(0, array.shape[1], units)]
    while len(parts) > 1:
        parts = [a + b for a, b in zip(parts[::2], parts[1::2])]
    return parts[0]


def lane_start(value):
    return pl.multiple_of(value, LANES)


def own_place():
    group, owner = lax.axis_index("grp"), lax.axis_index("dp")
    return lax.rem(group, 2), group // 2, lax.rem(owner, 2), owner // 2


def part_columns(place, width, side, chunk):
    core, plane = place[:2]
    core = core if side == 0 else 1 - core
    first = core * (width // 2) + chunk * (width // 4)
    small = width // 16
    offsets = (1 - plane, plane, 2 + plane, 3 - plane)
    return [lane_start(first + offset * small) for offset in offsets]


def weight_pieces(place, width, pieces):
    core, plane, x, z = place
    for index, (piece, blocks) in enumerate(pieces):
        if piece is None:
            yield index, 0, 0, 0
            continue
        far_core, far_plane, far_x, first = piece
        column = (1 - core if far_core else core) * (width // 2)
        column = column + (1 - plane if far_plane else plane) * (width // 4) + first
        for block in range(blocks):
            row = lax.rem(z - block + blocks, blocks) * 2 + (1 - x if far_x else x)
            yield index, block, row, lane_start(column)


TILE = 256
UNITS = 2


class Columns:
    def __init__(self, ref, first, rows):
        self.ref, self.first, self.shape = ref, first, (rows, ref.shape[0] * LANES)

    def tile(self, row, rows, column, lanes):
        row = self.first + row
        parts = [self.ref[at // LANES, row : row + rows, :] for at in range(column, column + lanes, LANES)]
        return jnp.concatenate(parts, axis=1)

    def all(self):
        return self.tile(0, self.shape[0], 0, self.shape[1])

    def store(self, row, column, value):
        for at in range(0, value.shape[1], LANES):
            rows = slice(self.first + row, self.first + row + value.shape[0])
            self.ref[(column + at) // LANES, rows, :] = value[:, at : at + LANES]


class ByHand:
    def __init__(self, weights, order, transpose, accumulators):
        self.weights, self.order, self.transpose = weights, order, transpose
        self.accumulators = accumulators

    def push(self, index):
        for unit in range(UNITS):
            rows, columns, _, _ = self.order[unit][index % len(self.order[unit])]
            tile = self.weights.tile(rows, TILE, columns, TILE)
            pltpu.matmul_push_rhs(tile, index % 2, unit, transpose=self.transpose)

    def begin(self, rows):
        self.push(0)
        self.push(1)
        self.load_first(rows)

    def load_first(self, rows):
        nothing = jnp.zeros((2 * rows, TILE), bf16)
        for unit in range(UNITS):
            pltpu.matmul_acc_lhs(self.accumulators[unit][0], nothing, load_staged_rhs=0)
        self.push(2)

    def multiply(self, left, index):
        for unit in range(UNITS):
            _, _, depth, column = self.order[unit][index]
            part = left[:, depth * TILE : (depth + 1) * TILE]
            staged = None if index == 0 else index % 2
            pltpu.matmul_acc_lhs(self.accumulators[unit][column], part, load_staged_rhs=staged)

    def pop(self, column):
        return [pltpu.matmul_pop(self.accumulators[unit][column]) for unit in range(UNITS)]

    def product(self, left):
        rows = left.shape[0]
        left = jnp.concatenate([left, jnp.zeros_like(left)], axis=0).astype(bf16)
        parts = []
        count = len(self.order[0])
        for index in range(count):
            self.multiply(left, index)
            if index > 0:
                self.push(index + 2)
            column = self.order[0][index][3]
            if index + 1 == count or self.order[0][index + 1][3] != column:
                parts += [part[:rows] for part in self.pop(column)]
        self.load_first(rows)
        return jnp.concatenate(parts, axis=1)

    def end(self, rows):
        left = jnp.zeros((2 * rows, TILE * (1 + max(entry[2] for entry in self.order[0]))), bf16)
        for index in range(3):
            self.multiply(left, index)
        for column in sorted({entry[3] for entry in self.order[0][:3]}):
            self.pop(column)


class ByCompiler:
    def __init__(self, weights, transpose):
        self.weights, self.transpose = weights, transpose

    def begin(self, rows):
        pass

    def product(self, left):
        dims = (((1,), (1 if self.transpose else 0,)), ((), ()))
        return lax.dot_general(left.astype(bf16), self.weights.all(), dims, preferred_element_type=f32)

    def end(self, rows):
        pass


def block_product(left_ref, weights, out):
    if not BY_HAND:
        out[...] = jnp.dot(left_ref[...], weights.all(), preferred_element_type=f32)
        return
    rows = left_ref.shape[0]
    depth, columns = weights.shape[0] // TILE, weights.shape[1] // TILE // UNITS
    count = depth * columns

    def body(accumulators):
        def tile(index, unit):
            return index % depth * TILE, (index // depth * UNITS + unit) * TILE

        def push(index):
            for unit in range(UNITS):
                row, column = tile(index, unit)
                part = weights.tile(row, TILE, column, TILE)
                pltpu.matmul_push_rhs(part, index % 2, unit)

        push(0)
        push(1)
        for index in range(count):
            for unit in range(UNITS):
                row, column = tile(index, unit)
                accumulator = accumulators[unit][index // depth % 2]
                pltpu.matmul_acc_lhs(accumulator, left_ref[:, row : row + TILE], load_staged_rhs=index % 2)
            if index + 2 < count:
                push(index + 2)
            if index % depth == depth - 1:
                for unit in range(UNITS):
                    row, column = tile(index, unit)
                    out[:, column : column + TILE] = pltpu.matmul_pop(accumulators[unit][index // depth % 2])

    pl.run_scoped(body, [[pltpu.ACC(unit)((rows, TILE), f32) for _ in range(2)] for unit in range(UNITS)])


def transpose(array, out):
    if not BY_HAND:
        out.store(0, 0, array.all().T)
        return
    high, columns = array.shape[0] // TILE // UNITS, array.shape[1] // TILE
    count = high * columns
    diagonal = lax.broadcasted_iota(jnp.int32, (TILE, TILE), 0) == lax.broadcasted_iota(
        jnp.int32, (TILE, TILE), 1
    )
    identity = jnp.where(diagonal, 1.0, 0.0).astype(bf16)

    def body(accumulators):
        def tile(index, unit):
            return (index // columns * UNITS + unit) * TILE, index % columns * TILE

        def push(index):
            for unit in range(UNITS):
                row, column = tile(index, unit)
                part = array.tile(row, TILE, column, TILE)
                pltpu.matmul_push_rhs(part, index % 2, unit, transpose=True)

        push(0)
        push(1)
        for index in range(count):
            for unit in range(UNITS):
                pltpu.matmul_acc_lhs(accumulators[unit][index % 2], identity, load_staged_rhs=index % 2)
            if index + 2 < count:
                push(index + 2)
            for unit in range(UNITS):
                row, column = tile(index, unit)
                part = pltpu.matmul_pop(accumulators[unit][index % 2])
                out.store(column, row, part.astype(bf16))

    pl.run_scoped(body, [[pltpu.ACC(unit)((TILE, TILE), f32) for _ in range(2)] for unit in range(UNITS)])


def matrix_product(body, weights, rows, transpose):
    if not BY_HAND:
        return body(ByCompiler(weights, transpose))
    high, wide_ = weights.shape
    depth, columns = (wide_ // TILE, high // TILE) if transpose else (high // TILE, wide_ // TILE)
    order = []
    for unit in range(UNITS):
        places = [(k, column) for column in range(columns // UNITS) for k in range(depth)]
        entries = []
        for k, column in places:
            at = (k * TILE, (column * UNITS + unit) * TILE)
            entries.append((*(at[::-1] if transpose else at), k, column))
        order.append(entries)
    shapes = [
        [pltpu.ACC(unit)((2 * rows, TILE), f32) for _ in range(columns // UNITS)] for unit in range(UNITS)
    ]
    return pl.run_scoped(
        lambda accumulators: body(ByHand(weights, order, transpose, accumulators)), shapes
    )


def sweep_kernel(
    rows,
    blocks,
    pieces,
    *refs,
):
    place = own_place()
    piece_refs, refs = refs[: len(pieces)], refs[len(pieces) :]
    (
        xb_ref,
        top_ref,
        cot_ref,
        bound_ref,
        z0_ref,
        h0_ref,
        c0_ref,
        small_ref,
        left_ref,
        hidden_ref,
        clast_ref,
        bounds_ref,
        w_parts_ref,
        own0_ref,
        own1_ref,
        other0_ref,
        other1_ref,
        dl_ref,
        gsmall_ref,
        w_ref,
        wt_s,
        xhat_s,
        gate_s,
        ftop_s,
        cell_s,
        tanh_s,
        hprev_s,
        bound_s,
        ds_s,
        zpre_s,
        zpost_s,
        rstd_s,
        rin_s,
        rtop_s,
        gain_s,
        gain_half_s,
        bias_half_s,
        vrec_s,
        wbar_s,
        sgain_s,
        sbias_s,
        svec_s,
        h_s,
        c_s,
        z_s,
        seq_s,
        in_sems,
        out_sems,
    ) = refs
    units = xb_ref.shape[1]
    width = w_ref.shape[0] * LANES
    tiles = units // LANES
    gate_tiles = width // LANES
    tokens = xb_ref.shape[0]
    pairs = tokens // (2 * rows)
    now = pl.program_id(0)
    forward = now < blocks
    block = jnp.where(forward, now, 2 * blocks - 1 - now)
    base = pl.multiple_of(block * tokens, tokens)
    part_refs = (own0_ref, own1_ref, other0_ref, other1_ref)
    part_blocks = [
        start // LANES for index in range(4) for start in part_columns(place, width, index // 2, index % 2)
    ]
    write_out = [
        pltpu.make_async_copy(
            w_ref.at[index, pl.ds(0, units), :], w_parts_ref.at[:, pl.ds(at * LANES, LANES)], out_sems.at[at]
        )
        for at, index in enumerate(part_blocks)
    ]

    lane = lax.broadcasted_iota(jnp.int32, (rows, LANES), 1)

    def vector(index):
        first = 2 * width + index * units
        return small_ref[:, first : first + units]

    @pl.when(now == 0)
    def _():
        copies = []
        for index, part, row, column in weight_pieces(place, width, pieces):
            ref = piece_refs[index]
            _, deep, lanes = ref.shape
            row = row * deep if isinstance(row, int) else pl.multiple_of(row * deep, deep)
            for at in range(lanes // LANES):
                source = ref.at[part, :, pl.ds(at * LANES, LANES)]
                into = w_ref.at[column // LANES + at, pl.ds(row, deep), :]
                copies.append(pltpu.make_async_copy(source, into, in_sems.at[len(copies)]))
        for copy in copies:
            copy.start()
        gain = jnp.broadcast_to(small_ref[:, :width], (rows, width))
        bias = jnp.broadcast_to(small_ref[:, width : 2 * width], (rows, width))
        split = 3 * units
        gain_s[...] = gain
        gain_half_s[:, :split] = (0.5 * width**0.5) * gain[:, :split]
        gain_half_s[:, split:] = width**0.5 * gain[:, split:]
        bias_half_s[:, :split] = 0.5 * bias[:, :split]
        bias_half_s[:, split:] = bias[:, split:]
        vrec_s[...] = jnp.broadcast_to(vector(1), (rows, units))
        h_s[...] = h0_ref[...]
        c_s[...] = c0_ref[...]
        row = lax.broadcasted_iota(jnp.int32, (rows, rows), 0)
        same = row == lax.broadcasted_iota(jnp.int32, (rows, rows), 1)
        z0 = jnp.where(same, jnp.broadcast_to(z0_ref[...], (rows, rows)), 0.0)
        z_s[...] = jnp.broadcast_to(lane_sum(z0), z_s.shape)
        seq_s[...] = jnp.zeros_like(seq_s)
        for copy in copies:
            copy.wait()
        for copy in write_out:
            copy.start()

        def row_means(matrix):
            matrix.begin(rows)
            wbar_s[...] = matrix.product(jnp.full((rows, width), 1.0 / width, f32))
            matrix.end(rows)

        matrix_product(row_means, Columns(w_ref, units, units), rows, True)

    def forward_step(matrix, local, h, c, z):
        at = pl.ds(pl.multiple_of(base + local, rows), rows)
        rec = matrix.product(h)
        low_f = h.astype(bf16).astype(f32)
        given = xhat_s[at, :] + wide(z, gate_tiles) * ftop_s[at, :]
        mean = lane_sum(low_f * wbar_s[...] + fold(given, units) * (1.0 / width))
        reach = lane_sum(low_f * vrec_s[...])
        b = bound_s[at, :]
        s = rec + (given - mean)
        squares = s * s
        parts = [fold(squares[:, at : at + units], LANES) for at in range(0, width, units)]
        root = lax.rsqrt(lane_sum(functools.reduce(jnp.add, parts)) + width * 1e-05)
        rstd = root * width**0.5
        half = (s * gain_half_s[...]) * root + bias_half_s[...]
        copied = (1.0 - z) * (1.0 - b)
        kept = (1.0 - z) * b
        fresh = wide(0.5 * (z + kept), tiles)
        half_c = wide(0.5 * kept, tiles) * c
        rest_c = half_c + wide(copied, tiles) * c
        gates = jnp.tanh(half)
        forget, inward, outward, candidate = (gates[:, k * units : (k + 1) * units] for k in range(4))
        c_next = (fresh * inward + fresh) * candidate + (forget * half_c + rest_c)
        th = jnp.tanh(c_next)
        forget, inward, outward = (0.5 * gate + 0.5 for gate in (forget, inward, outward))
        h_next = (wide(1.0 - copied, tiles) * outward) * th + wide(copied, tiles) * h
        z_next = half_sigmoid(0.5 * (rin_s[at, :] + reach + z * rtop_s[at, :]))
        xhat_s[at, :] = s * rstd
        gate_s[at, :units] = forget
        gate_s[at, units : 2 * units] = inward
        gate_s[at, 2 * units : 3 * units] = outward
        gate_s[at, 3 * units :] = candidate
        cell_s[at, :] = c
        tanh_s[at, :] = th
        hprev_s[at, :] = h
        zpre_s[at, :] = z
        zpost_s[at, :] = z_next
        rstd_s[at, :] = jnp.broadcast_to(rstd, z.shape)
        return h_next, c_next, z_next

    @pl.when(forward)
    def _():
        at = pl.ds(base, tokens)
        block_product(xb_ref, Columns(w_ref, 0, units), xhat_s.at[at, :])
        block_product(top_ref, Columns(w_ref, 2 * units, units), ftop_s.at[at, :])
        left_ref[:, :units] = xb_ref[...]
        shape = (tokens, LANES)
        rin_s[at, :] = jnp.broadcast_to(lane_sum(xb_ref[...].astype(f32) * vector(0)), shape)
        rtop_s[at, :] = jnp.broadcast_to(lane_sum(top_ref[...].astype(f32) * vector(2)), shape)
        for index in range(tokens // rows):
            column = lane_sum(jnp.where(lane == block * (tokens // rows) + index, bound_ref[...], 0.0))
            here = pl.ds(pl.multiple_of(base + index * rows, rows), rows)
            bound_s[here, :] = jnp.broadcast_to(column, (rows, LANES))

        def pair(matrix, index, carry):
            h0, c0, z0, seq = carry
            local = pl.multiple_of(index * 2 * rows, 2 * rows)
            h1, c1, z1 = forward_step(matrix, local, h0, c0, z0)
            h2, c2, z2 = forward_step(matrix, local + rows, h1, c1, z1)
            both = pl.ds(local, 2 * rows)
            left_ref[both, units : 2 * units] = jnp.concatenate([h0, h1], axis=0).astype(bf16)
            hidden_ref[both, :] = jnp.concatenate([h1, h2], axis=0).astype(bf16)
            z_pair = wide(jnp.concatenate([z0, z1], axis=0), tiles)
            left_ref[both, 2 * units :] = (top_ref[both, :].astype(f32) * z_pair).astype(bf16)
            step = block * (2 * pairs) + 2 * index
            seq = jnp.where(lane == step, z1, jnp.where(lane == step + 1, z2, seq))
            return h2, c2, z2, seq

        def steps(matrix):
            matrix.begin(rows)
            start = (h_s[...], c_s[...], z_s[...], seq_s[...])
            h, c, z, seq = lax.fori_loop(0, pairs, functools.partial(pair, matrix), start, unroll=4)
            matrix.end(rows)
            h_s[...] = h
            c_s[...] = c
            z_s[...] = z
            seq_s[...] = seq

        matrix_product(steps, Columns(w_ref, units, units), rows, False)

    @pl.when(now == blocks)
    def _():
        clast_ref[...] = c_s[...]
        bounds_ref[...] = seq_s[...]
        for copy in write_out:
            copy.wait()
        transpose(Columns(w_ref, units, units), Columns(wt_s, 0, width))
        h_s[...] = jnp.zeros_like(h_s)
        c_s[...] = jnp.zeros_like(c_s)
        z_s[...] = jnp.zeros_like(z_s)
        sgain_s[...] = jnp.zeros_like(sgain_s)
        sbias_s[...] = jnp.zeros_like(sbias_s)
        svec_s[...] = jnp.zeros_like(svec_s)

    def backward_step(matrix, local, cot, xb, top, bh_known, bh_mat, bc, bz):
        at = pl.ds(pl.multiple_of(base + local, rows), rows)
        z = zpre_s[at, :]
        b = bound_s[at, :]
        z_next = zpost_s[at, :]
        copied = (1.0 - z) * (1.0 - b)
        kept = (1.0 - z) * b
        fresh = z + kept
        c = cell_s[at, :]
        th = tanh_s[at, :]
        h = hprev_s[at, :]
        forget = gate_s[at, :units]
        inward = gate_s[at, units : 2 * units]
        outward = gate_s[at, 2 * units : 3 * units]
        candidate = gate_s[at, 3 * units :]
        xhat = xhat_s[at, :]
        rstd = rstd_s[at, :]
        new = wide(1.0 - copied, tiles) * outward
        written = inward * candidate
        by_dh = new * (1.0 - th * th)
        by_out = new * (th * (1.0 - outward))
        by_dc = (
            wide(kept, tiles) * c * (forget * (1.0 - forget)),
            wide(fresh, tiles) * (written * (1.0 - inward)),
            wide(fresh, tiles) * (inward * (1.0 - candidate * candidate)),
        )
        gain = [gain_s[:, k * units : (k + 1) * units] for k in range(4)]
        dh_known = bh_known + cot
        dh = dh_known + bh_mat
        dc = (bc + dh_known * by_dh) + bh_mat * by_dh
        d_out = dh * by_out
        dx_out = dh_known * (by_out * gain[2]) + bh_mat * (by_out * gain[2])
        dn = jnp.concatenate([dc * by_dc[0], dc * by_dc[1], d_out, dc * by_dc[2]], axis=1)
        dx = jnp.concatenate(
            [dc * (by_dc[0] * gain[0]), dc * (by_dc[1] * gain[1]), dx_out, dc * (by_dc[2] * gain[3])], axis=1
        )
        rstd_wide = wide(rstd, gate_tiles)
        sum1 = lane_sum(fold(dx, units))
        sum2 = lane_sum(fold(dx * xhat, units))
        ds = (rstd_wide * dx - (rstd_wide * (1.0 / width)) * sum1) - (xhat * rstd_wide * (1.0 / width)) * sum2
        bh_mat = matrix.product(ds)
        d_logit = bz * (z_next * (1.0 - z_next))
        bh_known = wide(copied, tiles) * dh + wide(d_logit, tiles) * vrec_s[...]
        bc_next = dc * (wide(kept, tiles) * forget + wide(copied, tiles))
        by_z = dc * (written - wide(b, tiles) * (forget * c + written) - wide(1.0 - b, tiles) * c)
        by_z = by_z - wide(1.0 - b, tiles) * (dh * (h - outward * th))
        bz_next = lane_sum(fold(ds * ftop_s[at, :], units) + by_z) + d_logit * rtop_s[at, :]
        sgain_s[...] += dn * xhat
        sbias_s[...] += dn
        low = h.astype(bf16).astype(f32)
        svec_s[:, :units] += wide(d_logit, tiles) * xb
        svec_s[:, units : 2 * units] += wide(d_logit, tiles) * low
        svec_s[:, 2 * units :] += wide(d_logit * z, tiles) * top
        return ds, d_logit, (bh_known, bh_mat, bc_next, bz_next)

    @pl.when(jnp.logical_not(forward))
    def _():
        def pair(matrix, index, carry):
            local = pl.multiple_of((pairs - 1 - index) * 2 * rows, 2 * rows)
            both = pl.ds(local, 2 * rows)
            given = [ref[both, :].astype(f32) for ref in (cot_ref, xb_ref, top_ref)]
            seq, *carry = carry
            ds1, dl1, carry = backward_step(matrix, local + rows, *(array[rows:] for array in given), *carry)
            ds0, dl0, carry = backward_step(matrix, local, *(array[:rows] for array in given), *carry)
            ds = jnp.concatenate([ds0, ds1], axis=0).astype(bf16)
            for at in range(gate_tiles):
                ds_s[at, :, :] = ds[:, at * LANES : (at + 1) * LANES]
            for at, index in enumerate(part_blocks):
                part_refs[at // tiles][both, at % tiles * LANES : (at % tiles + 1) * LANES] = ds_s[index, :, :]
            step = (base + local) // rows
            seq = jnp.where(lane == step, dl0, jnp.where(lane == step + 1, dl1, seq))
            return (seq, *carry)

        def steps(matrix):
            matrix.begin(rows)
            start = (seq_s[...], h_s[...], jnp.zeros((rows, units), f32), c_s[...], z_s[...])
            seq, bh_known, bh_mat, bc, bz = lax.fori_loop(0, pairs, functools.partial(pair, matrix), start, unroll=4)
            matrix.end(rows)
            h_s[...] = bh_known + bh_mat
            c_s[...] = bc
            z_s[...] = bz
            seq_s[...] = seq

        matrix_product(steps, Columns(wt_s, 0, width), rows, False)

    @pl.when(now == 2 * blocks - 1)
    def _():
        dl_ref[...] = seq_s[...]
        gsmall_ref[...] = jnp.zeros_like(gsmall_ref)
        row = 0
        for ref in (sgain_s, sbias_s, svec_s):
            total = jnp.sum(ref[...], axis=0, keepdims=True)
            for at in range(0, total.shape[1], LANES):
                gsmall_ref[row : row + 1, :] = total[:, at : at + LANES]
                row += 1


def sweep(described, pieces, xb, top, cot, bounds, z0, h0, c0, small_params):
    tokens, units = xb.shape
    rows = h0.shape[0]
    width = 4 * units
    block = TIME_BLOCK * rows
    blocks = tokens // block
    small_rows = -(-small_params.shape[1] // (16 * LANES)) * 16

    def both_ways(lanes):
        return pl.BlockSpec((block, lanes), lambda i: (jnp.where(i < blocks, i, 2 * blocks - 1 - i), 0))

    def going(lanes):
        return pl.BlockSpec((block, lanes), lambda i: (jnp.minimum(i, blocks - 1), 0))

    def returning(lanes):
        return pl.BlockSpec((block, lanes), lambda i: (jnp.minimum(blocks - 1, 2 * blocks - 1 - i), 0))

    def whole(shape):
        return pl.BlockSpec(shape, lambda i: (0, 0))

    anywhere = pl.BlockSpec(memory_space=pl.ANY)
    outs = [
        (going(3 * units), (tokens, 3 * units), bf16),
        (going(units), (tokens, units), bf16),
        (whole((rows, units)), (rows, units), f32),
        (whole((rows, LANES)), (rows, LANES), f32),
        (anywhere, (units, width), bf16),
        *[(returning(units), (tokens, units), bf16)] * 4,
        (whole((rows, LANES)), (rows, LANES), f32),
        (whole((small_rows, LANES)), (small_rows, LANES), f32),
    ]
    constants = (bounds, z0, h0, c0, small_params)
    return pl.pallas_call(
        functools.partial(sweep_kernel, rows, blocks, described),
        grid=(2 * blocks,),
        in_specs=[anywhere] * len(pieces)
        + [both_ways(units), both_ways(units), returning(units)]
        + [whole(array.shape) for array in constants],
        out_specs=[spec for spec, _, _ in outs],
        out_shape=[jax.ShapeDtypeStruct(shape, dtype) for _, shape, dtype in outs],
        scratch_shapes=[
            pltpu.VMEM((width // LANES, 3 * units, LANES), bf16),
            pltpu.VMEM((units // LANES, width, LANES), bf16),
            *[pltpu.VMEM((tokens, width), f32)] * 3,
            *[pltpu.VMEM((tokens, units), f32)] * 3,
            pltpu.VMEM((tokens, LANES), f32),
            pltpu.VMEM((width // LANES, 2 * rows, LANES), bf16),
            *[pltpu.VMEM((tokens, LANES), f32)] * 5,
            *[pltpu.VMEM((rows, width), f32)] * 3,
            *[pltpu.VMEM((rows, units), f32)] * 2,
            *[pltpu.VMEM((rows, width), f32)] * 2,
            pltpu.VMEM((rows, 3 * units), f32),
            *[pltpu.VMEM((rows, units), f32)] * 2,
            *[pltpu.VMEM((rows, LANES), f32)] * 2,
            pltpu.SemaphoreType.DMA((sum(piece.shape[0] * piece.shape[2] // LANES for piece in pieces),)),
            pltpu.SemaphoreType.DMA((width // LANES,)),
        ],
        compiler_params=pltpu.CompilerParams(
            dimension_semantics=("arbitrary",), vmem_limit_bytes=VMEM_LIMIT
        ),
        cost_estimate=pl.CostEstimate(flops=130 * 10**9, bytes_accessed=10**8, transcendentals=0),
        name="sweep",
    )(*pieces, xb, top, cot, *constants)


def adam_kernel(chunk, *refs):
    grads, (w_ref, m_ref, v_ref), (*outs, new_s, sems) = refs[:4], refs[4:7], refs[-5:]
    core, plane, _, _ = own_place()
    quarter = w_ref.shape[1] // 4
    copies = []
    for side in range(2):
        start = (1 - core if side else core) * (2 * quarter) + chunk * quarter
        for far_plane in range(2):
            grad_ref = grads[2 * side + far_plane]
            lanes = grad_ref.shape[1] // 2
            for half in range(2):
                at = (2 * half + (1 - plane if far_plane else plane)) * lanes
                columns = pl.ds(lane_start(start + at), lanes)
                grad = grad_ref[:, half * lanes : (half + 1) * lanes].astype(f32)
                new = adam_update(
                    w_ref[:, columns], grad, m_ref[:, columns], v_ref[:, columns], weight_rate, decay_rate
                )
                for index, value in enumerate(new):
                    new_s[index, side, :, pl.ds(lane_start(at), lanes)] = value
        for index, ref in enumerate(outs):
            into = ref.at[:, pl.ds(lane_start(start), quarter)]
            copies.append(pltpu.make_async_copy(new_s.at[index, side], into, sems.at[index, side]))
            copies[-1].start()
    for copy in copies:
        copy.wait()


def adam_columns(chunk, grads, master, first_moment, second_moment, earlier):
    rows, width = master.shape
    in_vmem, anywhere = pl.BlockSpec(memory_space=pltpu.VMEM), pl.BlockSpec(memory_space=pl.ANY)
    return pl.pallas_call(
        functools.partial(adam_kernel, chunk),
        in_specs=[in_vmem] * 7 + [anywhere] * len(earlier),
        out_specs=[anywhere] * 3,
        out_shape=[jax.ShapeDtypeStruct(master.shape, f32)] * 3,
        scratch_shapes=[pltpu.VMEM((3, 2, rows, width // 4), f32), pltpu.SemaphoreType.DMA((3, 2))],
        input_output_aliases={7 + k: k for k in range(len(earlier))},
        compiler_params=pltpu.CompilerParams(vmem_limit_bytes=SMALL_VMEM),
        name="adam",
    )(*grads, master, first_moment, second_moment, *earlier)


def after(value, others):
    return lax.optimization_barrier((value, others))[0]


def swap(array, bit, axis="grp"):
    count = lax.axis_size(axis)
    return lax.ppermute(array, axis, [(index, index ^ bit) for index in range(count)])


def along_z(array, step):
    count = lax.axis_size("dp")
    return lax.ppermute(array, "dp", [(index, (index + 2 * step) % count) for index in range(count)])


def gather_weights(shard, core, plane, ready):
    width = shard.shape[1]
    count = lax.axis_size("dp")
    if count != Z_SIZE * 2:
        return (None,), (lax.all_gather(shard.astype(bf16), "dp", axis=0, tiled=True)[None],)
    quarter = width // 4
    lanes = quarter // 2
    half = lanes // 2
    firsts = (0, lanes)
    owns = [
        lax.dynamic_slice_in_dim(
            shard, core * (width // 2) + plane * quarter + first, lanes, axis=1
        ).astype(bf16)
        for first in firsts
    ]

    def line(own):
        return tuple(along_z(own, step) for step in range(1, Z_SIZE))

    def planes(own, arrived):
        mine = jnp.stack((own,) + arrived)
        return mine, swap(mine, 1, "dp"), swap(mine, PLANE)

    def corners(pieces):
        return pieces[1][..., :half], pieces[2][..., half:]

    def corner_swap(from_x, from_y):
        return swap(from_x, PLANE), swap(from_y, 1, "dp")

    arrived0 = line(owns[0])
    own1 = after(owns[1], arrived0)
    arrived1 = line(own1)
    pieces0 = planes(owns[0], after(arrived0, ready))
    corners0 = corners(pieces0)
    pieces1 = planes(own1, after(arrived1, corners0))
    corners1 = corners(pieces1)
    all_pieces = [pieces0 + corner_swap(*corners0), pieces1 + corner_swap(*corners1)]
    kinds, pieces = [], []
    for first, here in zip(firsts, all_pieces):
        for far_core in (False, True):
            kinds += [
                (far_core, False, False, first),
                (far_core, False, True, first),
                (far_core, True, False, first),
                (far_core, True, True, first),
                (far_core, True, True, first + half),
            ]
            pieces += [swap(piece, CORE) for piece in after(here, corners1)] if far_core else here
    return tuple(kinds), tuple(pieces)


def split(value):
    high = value.astype(bf16)
    return high, (value - high.astype(f32)).astype(bf16)


def joined(high, low):
    return high.astype(f32) + low.astype(f32)


def both_parts(value):
    return joined(*split(value))


def small_call(kernel, arrays, extra, outs, extra_out=False):
    arrays = [*arrays, *extra]
    if extra_out:
        outs = outs + [(array.shape, array.dtype) for array in extra]
    return pl.pallas_call(
        functools.partial(kernel, len(extra)),
        in_specs=[pl.BlockSpec(memory_space=pltpu.VMEM)] * len(arrays),
        out_specs=[pl.BlockSpec(memory_space=pltpu.VMEM)] * len(outs),
        out_shape=[jax.ShapeDtypeStruct(shape, dtype) for shape, dtype in outs],
        compiler_params=pltpu.CompilerParams(vmem_limit_bytes=SMALL_VMEM),
        name=kernel.__name__,
    )(*arrays)


def first_kernel(with_small, total_ref, *refs):
    small_refs, (to_y_ref, to_x_ref) = refs[:with_small], refs[with_small:]
    _, _, x, _ = own_place()
    _, _, rows, columns = total_ref.shape
    small = columns // 4
    for index in range(2 * Z_SIZE):
        to_y_ref[index * rows : (index + 1) * rows, :] = total_ref[index // 2, index % 2, :, :small].astype(bf16)
    if with_small:
        deep = small_refs[0].shape[0]
        start = 2 * Z_SIZE * rows
        high, low = split(small_refs[0][...])
        to_y_ref[start : start + deep, :] = high
        to_y_ref[start + deep :, :] = low
    to_x_ref[...] = total_ref[:, 1 - x, :, 2 * small :].astype(bf16)


def second_kernel(with_small, total_ref, from_y_ref, from_x_ref, *refs):
    small_refs, (to_x_ref, to_y_ref, kept_ref, *small_outs) = refs[:with_small], refs[with_small:]
    _, _, x, _ = own_place()
    _, _, rows, columns = total_ref.shape
    small = columns // 4
    middle = slice(small, 2 * small)

    def from_y(index, of_x):
        start = (2 * index + of_x) * rows
        if rows % 16 == 0:
            start = pl.multiple_of(start, 16)
        return from_y_ref[pl.ds(start, rows), :].astype(f32)

    for index in range(Z_SIZE):
        away = total_ref[index, 1 - x, :, middle] + from_y(index, 1 - x)
        to_x_ref[index * rows : (index + 1) * rows, :] = away.astype(bf16)
        kept_ref[index, :, :small] = total_ref[index, x, :, middle] + from_y(index, x)
    right = total_ref[:, x, :, 2 * small :] + from_x_ref[...].astype(f32)
    kept_ref[..., small:] = right[..., :small]
    to_y_ref[...] = right[..., small:].astype(bf16)
    if with_small:
        deep = small_refs[0].shape[0]
        start = 2 * Z_SIZE * rows
        arrived = joined(from_y_ref[start : start + deep, :], from_y_ref[start + deep :, :])
        value = both_parts(small_refs[0][...]) + arrived
        small_outs[0][...] = value
        start = Z_SIZE * rows
        high, low = split(value)
        to_x_ref[start : start + deep, :] = high
        to_x_ref[start + deep :, :] = low


def third_kernel(with_small, kept_ref, from_x_ref, from_y_ref, *refs):
    small_refs, (own_ref, *away_refs) = refs[:with_small], refs[with_small:]
    _, _, _, z = own_place()
    _, rows, columns = kept_ref.shape
    small = columns // 2
    small_outs, away_refs = away_refs[Z_SIZE - 1 :], away_refs[: Z_SIZE - 1]
    for step, ref in enumerate([own_ref] + away_refs):
        at = lax.rem(z + step, Z_SIZE)
        start = at * rows
        if rows % 16 == 0:
            start = pl.multiple_of(start, 16)
        left = kept_ref[at, :, :small] + from_x_ref[pl.ds(start, rows), :].astype(f32)
        ref[:rows, :small] = left.astype(ref.dtype)
        ref[:rows, small:] = (kept_ref[at, :, small:] + from_y_ref[at].astype(f32)).astype(ref.dtype)
    if with_small:
        deep = small_refs[0].shape[0]
        start = Z_SIZE * rows
        arrived = joined(from_x_ref[start : start + deep, :], from_x_ref[start + deep :, :])
        value = both_parts(small_refs[0][...]) + arrived
        small_outs[0][...] = value
        high, low = split(value)
        for ref in away_refs:
            ref[rows:, :small] = high
            ref[rows:, small:] = low


def fourth_kernel(with_small, own_ref, *refs):
    arrived, refs = refs[: Z_SIZE - 1], refs[Z_SIZE - 1 :]
    small_refs, (out_ref, *small_outs) = refs[:with_small], refs[with_small:]
    rows, columns = own_ref.shape
    small = columns // 2
    total = own_ref[...]
    for ref in arrived:
        total = total + ref[:rows, :].astype(f32)
    out_ref[...] = total.astype(bf16)
    if with_small:
        one, two, three = (joined(ref[rows:, :small], ref[rows:, small:]) for ref in arrived)
        value = (both_parts(small_refs[0][...]) + two) + (one + three)
        small_outs[0][:, :small], small_outs[0][:, small:] = split(value)


def reduce_rows(totals, grad_small, late, late_inputs):
    count = lax.axis_size("dp")
    all_rows, columns = totals[0].shape
    small = columns // 4
    deep = grad_small.shape[0]
    if count != Z_SIZE * 2:
        sums = []
        for total in totals:
            mine = lax.psum_scatter(total.astype(bf16), "dp", scatter_dimension=0, tiled=True).astype(f32)
            away = jnp.concatenate([mine[:, :small], mine[:, 3 * small :]], axis=1).astype(bf16)
            sums.append((mine[:, small : 3 * small] + swap(away, PLANE).astype(f32)).astype(bf16))
        total = grad_small + swap(grad_small, PLANE)
        bit = 1
        while bit < count:
            total = total + swap(total, bit, "dp")
            bit *= 2
        return sums, jnp.concatenate(split(total), axis=1), late(*late_inputs)
    rows = all_rows // count
    totals = [total.reshape(Z_SIZE, 2, rows, columns) for total in totals]

    def first(total, extra):
        below = 2 * deep if extra else 0
        outs = [((2 * Z_SIZE * rows + below, small), bf16), ((Z_SIZE, rows, 2 * small), bf16)]
        return small_call(first_kernel, [total], extra, outs)

    def first_swap(to_y, to_x):
        return swap(to_y, PLANE), swap(to_x, 1, "dp")

    def second(total, arrived, extra):
        below = 2 * deep if extra else 0
        outs = [
            ((Z_SIZE * rows + below, small), bf16),
            ((Z_SIZE, rows, small), bf16),
            ((Z_SIZE, rows, 2 * small), f32),
        ]
        return small_call(second_kernel, [total, *arrived], extra, outs, True)

    def second_swap(to_x, to_y, kept):
        return kept, swap(to_x, 1, "dp"), swap(to_y, PLANE)

    def third(arrived, extra):
        below = deep if extra else 0
        outs = [((rows, 2 * small), f32)] + [((rows + below, 2 * small), bf16)] * (Z_SIZE - 1)
        return small_call(third_kernel, arrived, extra, outs, True)

    def third_swap(own, *away):
        return (own,) + tuple(along_z(array, step + 1) for step, array in enumerate(away))

    def fourth(arrived, extra):
        outs = [((rows, 2 * small), bf16)] + [((deep, 2 * small), bf16)] * len(extra)
        return small_call(fourth_kernel, arrived, extra, outs)

    extra = [grad_small]
    out0 = first(totals[0], extra)
    in0 = first_swap(*out0)
    out1 = first(totals[1], [])
    in1 = first_swap(*out1)
    *out0, value = second(totals[0], in0, extra)
    extra = [value]
    in0 = second_swap(*out0)
    out1 = second(totals[1], after(in1, out0), [])
    in1 = second_swap(*out1)
    *out0, value = third(after(in0, out1), extra)
    extra = [value]
    in0 = third_swap(*out0)
    out1 = third(after(in1, out0), [])
    late_outputs = late(*after(late_inputs, out1))
    in1 = third_swap(*out1)
    sum0, small_pair = fourth(after(in0, (late_outputs, in1[1])), extra)
    (sum1,) = fourth(after(in1, sum0), [])
    return [sum0, sum1], small_pair, late_outputs


def shards(
    inputs,
    top_down,
    lower_bounds,
    h_init,
    c_init,
    z_init,
    out_cot,
    gate_weight,
    gate_m,
    gate_v,
    small_params,
    small_m,
    small_v,
):
    rows, steps, units = inputs.shape
    tokens = rows * steps
    width = 4 * units
    core, plane, _, _ = own_place()

    def by_time(array):
        return jnp.swapaxes(array, 0, 1).reshape((tokens,) + array.shape[2:])

    def by_window(array):
        return jnp.swapaxes(array.reshape((steps, rows) + array.shape[1:]), 0, 1)

    bound = by_time(lower_bounds).astype(f32)
    ready = (
        by_time(inputs) * bound[:, None].astype(bf16),
        by_time(top_down),
        by_time(out_cot),
        jnp.pad(lower_bounds.astype(f32), ((0, 0), (0, LANES - steps))),
        z_init[None],
        small_params[None],
    )
    kinds, pieces = gather_weights(gate_weight, core, plane, ready)
    described = tuple((kind, piece.shape[0]) for kind, piece in zip(kinds, pieces))
    xb, top, cot, bounds_f, z0, small_row = ready
    left, hidden, c_last, bounds, w_parts, own0, own1, other0, other1, d_logit, grad_small = sweep(
        described, pieces, xb, top, cot, bounds_f, z0, h_init, c_init, small_row
    )

    def product(right):
        return lax.dot_general(left, right, (((0,), (0,)), ((), ())), preferred_element_type=f32)

    totals = []
    for own, other in ((own0, other0), (own1, other1)):
        from_core = swap(product(other).astype(bf16), CORE)
        totals.append(product(own) + from_core.astype(f32))
    v_input = small_params[2 * width : 2 * width + units]

    def late(d_logit, hidden, *parts):
        by_input = 0.0
        for index, part in enumerate(parts):
            columns = w_parts[:, index * units : (index + 1) * units]
            by_input = by_input + lax.dot_general(
                part, columns, (((1,), (1,)), ((), ())), preferred_element_type=f32
            )
        by_logit = lower_bounds.astype(f32) * d_logit[:, :steps]
        input_grad = by_window(bound[:, None] * by_input) + by_logit[:, :, None] * v_input
        return by_window(hidden), input_grad

    late_inputs = d_logit, hidden, own0, own1, other0, other1
    sums, small_pair, (hidden, input_grad) = reduce_rows(totals, grad_small, late, late_inputs)
    weights = ()
    for chunk, grad in enumerate(sums):
        grads = [grad] + [swap(grad, bits) for bits in (PLANE, CORE, CORE | PLANE)]
        weights = adam_columns(chunk, grads, gate_weight, gate_m, gate_v, weights)
    weight_new, weight_m, weight_v = weights
    small_total = 0.0
    for pair in (small_pair, swap(small_pair, CORE)):
        small_total = small_total + joined(pair[:, :LANES], pair[:, LANES:])
    small_total = small_total.reshape(-1)[: small_params.shape[0]]

    small_new, small_m_new, small_v_new = adam_update(
        small_params, small_total, small_m, small_v, small_rate, 0.0
    )
    return (
        hidden,
        c_last,
        bounds[:, :steps],
        input_grad,
        weight_new,
        weight_m,
        weight_v,
        small_new,
        small_m_new,
        small_v_new,
    )


def solution(mesh):
    def program(*arrays):
        with jax.sharding.use_abstract_mesh(mesh.abstract_mesh):
            return sharded(*arrays)

    tokens = P(("dp", "grp"), None, None)
    windows = P(("dp", "grp"), None)
    owned = P("dp", None)
    in_specs = (
        (tokens, tokens, windows, windows, windows, P(("dp", "grp")), tokens)
        + (owned,) * 3
        + (P(),) * 3
    )
    out_specs = (tokens, windows, windows, tokens) + (owned,) * 3 + (P(),) * 3
    sharded = jax.shard_map(shards, mesh=mesh, in_specs=in_specs, out_specs=out_specs, check_vma=False)
    return program
```
